256 devices in a mesh: ta: 16 (over x_lo, z), gz: 2 (over core), gy: 4 (over y), gx: 2 (over x_hi).
Axes of the slice: x: 4 (x_hi: 2, x_lo: 2; x = x_hi * 2 + x_lo), y: 4, z: 8, core: 2. Of those that a mesh axis runs over, the one named last changes fastest.
Arguments:
- source: float32 [2, 4, 3, 16, 2, 4, 8, 256], P(None, None, None, 'ta', 'gz', 'gy', 'gx'), may hold values from -6 to 6
- gauge_links: bfloat16 [4, 2, 3, 3, 16, 2, 4, 8, 256], P(None, None, None, None, 'ta', 'gz', 'gy', 'gx'), may hold values from -2.5 to 2.5
- clover_inverse: bfloat16 [2, 2, 6, 6, 16, 2, 4, 8, 256], P(None, None, None, None, 'ta', 'gz', 'gy', 'gx'), may hold values from -0.5 to 1.5, as said below
- vectors: bfloat16 [16, 2, 4, 3, 16, 2, 4, 8, 256], P(None, None, None, None, 'ta', 'gz', 'gy', 'gx'), may hold values from -0.75 to 0.75
- coarse_hops: float32 [8, 2, 16, 16, 16, 2, 4, 8], P(None, None, None, None, 'ta', 'gz', 'gy', 'gx'), may hold values from -0.25 to 0.25
Outputs:
- solution: float32 [2, 4, 3, 16, 2, 4, 8, 256], P(None, None, None, 'ta', 'gz', 'gy', 'gx')
- coarse_error: float32 [2, 16, 16, 2, 4, 8], P(None, None, 'ta', 'gz', 'gy', 'gx')
The draws below stay inside these ranges and needn't reach their ends.
Inputs may be any that keep to these rules, and one draw needn't show every extreme that they name: `clover_inverse`: each chirality block is hermitian.
All inputs are finite; a program needn't handle non-finite values.
Results may differ from the reference program's by a relative error of at most 0.0029.
Values sent between devices are 32-bit elements; how exact they have to be, the bound alone decides.
A program may use at most 128 MiB of HBM per device.

```python
import jax
import jax.numpy as jnp
import numpy as np
from jax import lax

EDGE = 4
BLOCK = 256
NV = 16
NBT = 16
NBZ = 2
NBY = 4
NBX = 8


def draw_clover_inverse(key, part):
    key = jax.random.fold_in(key, 11)
    diagonal_key, real_key, imag_key = jax.random.split(key, 3)
    tail_shape = (NBT, NBZ, NBY, NBX, BLOCK)
    diagonal = jax.random.uniform(diagonal_key, (2, 6) + tail_shape, jnp.float32, 0.6, 1.0)
    real_noise = jnp.clip(jax.random.normal(real_key, (2, 6, 6) + tail_shape, jnp.float32), -4.0, 4.0) * 0.11
    imag_noise = jnp.clip(jax.random.normal(imag_key, (2, 6, 6) + tail_shape, jnp.float32), -4.0, 4.0) * 0.11
    real_part = 0.5 * (real_noise + jnp.swapaxes(real_noise, 1, 2))
    imag_part = 0.5 * (imag_noise - jnp.swapaxes(imag_noise, 1, 2))
    identity = jnp.eye(6, dtype=jnp.float32).reshape((1, 6, 6, 1, 1, 1, 1, 1))
    real_part = real_part + identity * diagonal[:, :, None]
    return jnp.stack([real_part, imag_part], axis=1).astype(jnp.bfloat16)


def steps_of(rng, dims, shards, least, top_value):
    factor_of, own = 1.0, jax.random.fold_in(rng, 6)
    for dim, blocks in shards:
        draws = jnp.exp(jax.random.uniform(jax.random.fold_in(own, dim), (blocks,), jnp.float32, least / len(shards), top_value / len(shards)))
        factor_of = factor_of * jnp.repeat(draws, dims[dim] // blocks).reshape([-1 if axis == dim else 1 for axis in range(len(dims))])
    return factor_of


def noise(key, extent, spread, limit, cuts=(), kind=jnp.bfloat16):
    level = steps_of(key, extent, cuts, -0.22, 0.18) if cuts else 1.0
    drawn = jax.random.normal(key, extent, jnp.float32) * spread * level
    return jnp.minimum(jnp.maximum(drawn, -limit), limit).astype(kind)


def setup_inputs(seed: int = 0) -> dict:
    seeds = jax.random.split(jax.random.key(seed), 6)
    return {
        "source": noise(seeds[0], (2, 4, 3, NBT, NBZ, NBY, NBX, BLOCK), 1.0, 6.0, ((3, 16), (4, 2), (5, 4), (6, 2)), jnp.float32),
        "gauge_links": noise(seeds[1], (4, 2, 3, 3, NBT, NBZ, NBY, NBX, BLOCK), 6 ** -0.5, 2.5, ((4, 16), (5, 2), (6, 4), (7, 2))),
        "clover_inverse": draw_clover_inverse(jax.random.fold_in(seeds[5], 71), 0),
        "vectors": noise(seeds[3], (NV, 2, 4, 3, NBT, NBZ, NBY, NBX, BLOCK), 64 ** -0.5, 0.75, ((4, 16), (5, 2), (6, 4), (7, 2))),
        "coarse_hops": noise(seeds[4], (8, 2, NV, NV, NBT, NBZ, NBY, NBX), 0.04, 0.25, ((4, 16), (5, 2), (6, 4), (7, 2)), jnp.float32),
    }


kappa_value = 0.125
fine_relax = 0.8
coarse_relax = 0.7


def real_form(real_part, imag_part):
    rows, columns = real_part.shape
    result = np.zeros((2 * rows, 2 * columns), np.float32)
    result[:rows, :columns] = real_part
    result[:rows, columns:] = -imag_part
    result[rows:, :columns] = imag_part
    result[rows:, columns:] = real_part
    return result


def side_by_side(sign, coupling_real, coupling_imag):
    real_part = np.zeros((2, 4), np.float32)
    imag_part = np.zeros((2, 4), np.float32)
    real_part[:, :2] = np.eye(2, dtype=np.float32)
    real_part[:, 2:] = sign * coupling_real
    imag_part[:, 2:] = sign * coupling_imag
    return real_form(real_part, imag_part)


def one_above(sign, coupling_real, coupling_imag):
    real_part = np.zeros((4, 2), np.float32)
    imag_part = np.zeros((4, 2), np.float32)
    real_part[:2, :] = np.eye(2, dtype=np.float32)
    real_part[2:, :] = sign * coupling_real
    imag_part[2:, :] = sign * coupling_imag
    return real_form(real_part, imag_part)


def spin_tables():
    zero_block = np.zeros((2, 2), np.float32)
    couplings = [(np.eye(2, dtype=np.float32), zero_block),
                 (zero_block, np.array([[-1.0, 0.0], [0.0, 1.0]], np.float32)),
                 (np.array([[0.0, -1.0], [1.0, 0.0]], np.float32), zero_block),
                 (zero_block, np.array([[0.0, -1.0], [-1.0, 0.0]], np.float32))]
    tables = []
    for coupling_real, coupling_imag in couplings:
        adjoint_real = coupling_real.T
        adjoint_imag = -coupling_imag.T
        tables.append((side_by_side(-1.0, coupling_real, coupling_imag), one_above(-1.0, adjoint_real, adjoint_imag),
                       side_by_side(1.0, coupling_real, coupling_imag), one_above(1.0, adjoint_real, adjoint_imag)))
    return tables


def layer_tables(direction):
    stride = EDGE ** (3 - direction)
    position = np.arange(EDGE ** 4)
    coordinate = (position // stride) % EDGE
    layer_position = np.arange(EDGE ** 3)
    lower_layer = (layer_position // stride) * (stride * EDGE) + layer_position % stride
    upper_layer = lower_layer + (EDGE - 1) * stride
    place_index = (position // (stride * EDGE)) * stride + position % stride
    return stride, lower_layer, upper_layer, place_index, coordinate == EDGE - 1, coordinate == 0


def apply_spin(spin_table, spinor):
    pairs = spinor.shape[1]
    flattened = spinor.reshape((2 * pairs,) + spinor.shape[2:])
    result = jnp.tensordot(jnp.asarray(spin_table), flattened, axes=1, precision=lax.Precision.HIGHEST)
    return result.reshape((2, spin_table.shape[0] // 2) + spinor.shape[2:])


def colour(matrix, vector):
    real_part = matrix[0].astype(jnp.float32)[None]
    imag_part = matrix[1].astype(jnp.float32)[None]
    vector_real = vector[0][:, None]
    vector_imag = vector[1][:, None]
    return jnp.stack([jnp.sum(real_part * vector_real - imag_part * vector_imag, axis=2),
                      jnp.sum(real_part * vector_imag + imag_part * vector_real, axis=2)])


def adjoint(matrix):
    return jnp.stack([jnp.swapaxes(matrix[0], 0, 1), -jnp.swapaxes(matrix[1], 0, 1)])


def hopping(spinor, gauge_links):
    summed = jnp.zeros_like(spinor)
    tables = spin_tables()
    for direction in range(4):
        project_minus, lift_minus, project_plus, lift_plus = tables[direction]
        stride, lower_layer, upper_layer, place_index, upper_mask, lower_mask = layer_tables(direction)
        block_axis = 3 + direction
        link_matrix = gauge_links[direction]
        forward_half = apply_spin(project_minus, spinor)
        backward_half = colour(adjoint(link_matrix), apply_spin(project_plus, spinor))
        next_layers = jnp.roll(jnp.take(forward_half, lower_layer, axis=-1), -1, axis=block_axis)
        prior_layers = jnp.roll(jnp.take(backward_half, upper_layer, axis=-1), 1, axis=block_axis)
        ahead_values = jnp.where(upper_mask, jnp.take(next_layers, place_index, axis=-1), jnp.roll(forward_half, -stride, axis=-1))
        behind = jnp.where(lower_mask, jnp.take(prior_layers, place_index, axis=-1), jnp.roll(backward_half, stride, axis=-1))
        summed = summed + apply_spin(lift_minus, colour(link_matrix, ahead_values)) + apply_spin(lift_plus, behind)
    return summed


def clover_apply(clover, spinor):
    pieces = []
    for chirality in range(2):
        half_spinor = spinor[:, 2 * chirality:2 * chirality + 2]
        flattened = half_spinor.reshape((2, 1, 6) + half_spinor.shape[3:])
        pieces.append(colour(clover[chirality], flattened).reshape(half_spinor.shape))
    return jnp.concatenate(pieces, axis=1)


def restrict(residual, vectors):
    rounded = residual.astype(jnp.bfloat16)
    stacked = jnp.stack([rounded, jnp.stack([rounded[1], -rounded[0]])])
    return jnp.einsum('krsctzyxi,jrsctzyxi->jktzyx', vectors.astype(jnp.float32), stacked.astype(jnp.float32),
                      precision=lax.Precision.HIGHEST)


def prolong(coarse_error, vectors):
    rounded = coarse_error.astype(jnp.bfloat16)
    parts = jnp.einsum('krsctzyxi,jktzyx->jrsctzyxi', vectors.astype(jnp.float32), rounded.astype(jnp.float32),
                       precision=lax.Precision.HIGHEST)
    return jnp.stack([parts[0, 0] - parts[1, 1], parts[0, 1] + parts[1, 0]])


def coarse_apply(coarse_error, coarse_hops):
    summed = coarse_error
    for direction in range(4):
        ahead_values = jnp.roll(coarse_error, -1, axis=2 + direction)
        behind = jnp.roll(coarse_error, 1, axis=2 + direction)
        summed = summed - colour(coarse_hops[2 * direction], ahead_values[:, None])[:, 0]
        summed = summed - colour(coarse_hops[2 * direction + 1], behind[:, None])[:, 0]
    return summed


def reference(source, gauge_links, clover_inverse, vectors, coarse_hops):
    def operator(spinor):
        return spinor - kappa_value * clover_apply(clover_inverse, hopping(spinor, gauge_links))

    iterate = fine_relax * source
    iterate = iterate + fine_relax * (source - operator(iterate))
    residual = source - operator(iterate)
    coarse_source = restrict(residual, vectors)
    coarse_error = coarse_relax * coarse_source
    coarse_error = coarse_error + coarse_relax * (coarse_source - coarse_apply(coarse_error, coarse_hops))
    iterate = iterate + prolong(coarse_error, vectors)
    for repeat in range(2):
        iterate = iterate + fine_relax * (source - operator(iterate))
    return iterate, coarse_error
```

```python
import jax
import jax.numpy as jnp
from jax import lax
from jax.experimental import pallas as pl
from jax.experimental.pallas import tpu as pltpu
from jax.sharding import PartitionSpec as P


kappa_value = 0.125
fine_relax = 0.8
coarse_relax = 0.7

F32 = jnp.float32
BF16 = jnp.bfloat16

B_ROWS = (((0, 0), (1, 0)), ((0, 3), (1, 1)), ((1, 2), (0, 0)), ((1, 3), (0, 3)))
B_ADJOINT_ROWS = (((0, 0), (1, 0)), ((0, 1), (1, 3)), ((1, 0), (0, 2)), ((1, 1), (0, 1)))

T_AHEAD, T_BEHIND, Y_AHEAD, Y_BEHIND, Z_BOTH, X_BOTH = 0, 3, 6, 9, 12, 18
TILES = 21


def plus_unit(target, unit, value):
    if unit == 0:
        return target[0] + value[0], target[1] + value[1]
    if unit == 1:
        return target[0] - value[1], target[1] + value[0]
    if unit == 2:
        return target[0] - value[0], target[1] - value[1]
    return target[0] + value[1], target[1] - value[0]


def project(spins, direction, sign):
    halves = []
    for row in range(2):
        column, unit = B_ROWS[direction][row]
        unit = unit if sign > 0 else (unit + 2) % 4
        halves.append(plus_unit(spins[row], unit, spins[2 + column]))
    return jnp.concatenate([halves[0][0], halves[1][0], halves[0][1], halves[1][1]], axis=0)


def lift(summed, half, direction, sign):
    pair = [(half[0:3], half[6:9]), (half[3:6], half[9:12])]
    result = []
    for row in range(2):
        result.append(plus_unit(summed[row], 0, pair[row]))
    for row in range(2):
        column, unit = B_ADJOINT_ROWS[direction][row]
        unit = unit if sign > 0 else (unit + 2) % 4
        result.append(plus_unit(summed[2 + row], unit, pair[column]))
    return result


def link_times(links, direction, half, dagger):
    real_part = half[:6].reshape(2, 3, 8, 128)
    imag_part = half[6:].reshape(2, 3, 8, 128)
    out_real = out_imag = None
    for b in range(3):
        if dagger:
            u_real, u_imag = links[direction, 0, b], links[direction, 1, b]
        else:
            u_real, u_imag = links[direction, 0, :, b], links[direction, 1, :, b]
        u_real, u_imag = u_real[None], u_imag[None]
        v_real, v_imag = real_part[:, b][:, None], imag_part[:, b][:, None]
        if dagger:
            term_real = u_real * v_real + u_imag * v_imag
            term_imag = u_real * v_imag - u_imag * v_real
        else:
            term_real = u_real * v_real - u_imag * v_imag
            term_imag = u_real * v_imag + u_imag * v_real
        out_real = term_real if out_real is None else out_real + term_real
        out_imag = term_imag if out_imag is None else out_imag + term_imag
    return jnp.concatenate([out_real.reshape(6, 8, 128), out_imag.reshape(6, 8, 128)], axis=0)


def lane_roll(values, shift):
    shift = shift % 128
    return values if shift == 0 else pltpu.roll(values, shift, values.ndim - 1)


def row_roll(values, shift):
    shift = shift % 8
    return values if shift == 0 else pltpu.roll(values, shift, values.ndim - 2)


class Places:
    def __init__(self):
        row = lax.broadcasted_iota(jnp.int32, (8, 128), 0)
        lane = lax.broadcasted_iota(jnp.int32, (8, 128), 1)
        self.row, self.lane = row, lane
        self.block = row % 4
        self.half = row // 4
        self.parity = lane // 64
        self.slot = {1: (lane // 16) % 4, 2: (lane // 4) % 4, 3: lane % 4}


STRIDE = {1: 16, 2: 4, 3: 1}


def choose(mask, first, second):
    return jnp.where(jnp.broadcast_to(mask[None], first.shape), first, second)


def pack_slots(half, direction, ahead, places):
    stride, slot = STRIDE[direction], places.slot[direction]
    fours = half.reshape(3, 4, 8, 128)
    packed = fours[:, 0]
    for k in range(1, 4):
        if ahead:
            packed = choose(slot == k, lane_roll(fours[:, k], stride * k), packed)
        else:
            packed = choose(slot == 3 - k, lane_roll(fours[:, k], -stride * k), packed)
    return packed


def merge_slots(rolled, packed, direction, ahead, places):
    stride, slot = STRIDE[direction], places.slot[direction]
    fours = rolled.reshape(3, 4, 8, 128)
    merged = []
    for k in range(4):
        if ahead:
            merged.append(choose(slot == 3, lane_roll(packed, stride * (3 - k)), fours[:, k]))
        else:
            merged.append(choose(slot == 0, lane_roll(packed, -stride * (3 - k)), fours[:, k]))
    return jnp.stack(merged, axis=1).reshape(12, 8, 128)


def pack_time(half, ahead, places):
    edge = places.parity == (0 if ahead else 1)
    edge_rows = places.half == (0 if ahead else 1)
    pairs = half.reshape(6, 2, 8, 128)
    first, second = pairs[:, 0], lane_roll(pairs[:, 1], 64)
    paired = choose(edge, first, second).reshape(3, 2, 8, 128)
    paired_first, paired_second = paired[:, 0], row_roll(paired[:, 1], 4)
    packed = choose(edge_rows, paired_first, paired_second)
    return packed, (first, second, paired_first, paired_second)


def merge_time(state, packed, ahead, places):
    edge = places.parity == (0 if ahead else 1)
    edge_rows = places.half == (0 if ahead else 1)
    first, second, paired_first, paired_second = state
    next_first = row_roll(choose(edge_rows, packed, paired_first), 4)
    next_second = choose(edge_rows, paired_second, packed)
    moved = jnp.stack([next_first, next_second], axis=1).reshape(6, 8, 128)
    out_first = lane_roll(choose(edge, moved, first), 64)
    out_second = choose(edge, second, moved)
    return jnp.stack([out_first, out_second], axis=1).reshape(12, 8, 128)


def spins_of(values):
    return [(values[3 * s : 3 * s + 3], values[12 + 3 * s : 15 + 3 * s]) for s in range(4)]


def tiles_of(spins):
    return jnp.concatenate([spin[0] for spin in spins] + [spin[1] for spin in spins], axis=0)


def kernel(
    source_hbm,
    links_hbm,
    clover_hbm,
    vectors_hbm,
    hops_hbm,
    out_ref,
    coarse_ref,
    source_ref,
    links_raw,
    clover_raw,
    vectors_raw,
    hops_ref,
    links,
    clover,
    matrix,
    scaled,
    send_buffer,
    recv_buffer,
    coarse_send,
    coarse_recv,
    load_sem,
    send_sem,
    recv_sem,
    coarse_send_sem,
    coarse_recv_sem,
):
    loads = []
    for index, (origin, target) in enumerate(
        (
            (source_hbm, source_ref),
            (links_hbm, links_raw),
            (clover_hbm, clover_raw),
            (vectors_hbm, vectors_raw),
            (hops_hbm, hops_ref),
        )
    ):
        loads.append(pltpu.make_async_copy(origin, target, load_sem.at[index]))
        loads[-1].start()

    def around(axis, step):
        count = lax.axis_size(axis)
        return {axis: lax.rem(lax.axis_index(axis) + (step + count), count)}

    t_next, t_prior = around("ta", 1), around("ta", -1)
    y_next, y_prior = around("gy", 1), around("gy", -1)
    z_other, x_other = around("gz", 1), around("gx", 1)

    barrier = pltpu.get_barrier_semaphore()
    for neighbour in (t_next, t_prior, y_next, y_prior, z_other, x_other):
        pl.semaphore_signal(
            barrier, inc=1, device_id=neighbour, device_id_type=pl.DeviceIdType.MESH
        )

    places = Places()

    def message(sweep, number, start, count, target):
        window = pl.ds(start, count)
        return pltpu.make_async_remote_copy(
            src_ref=send_buffer.at[sweep, window],
            dst_ref=recv_buffer.at[sweep, window],
            send_sem=send_sem.at[sweep, number],
            recv_sem=recv_sem.at[sweep, number],
            device_id=target,
            device_id_type=pl.DeviceIdType.MESH,
        )

    started = []

    def clover_hopping(sweep, psi, before_send=None, while_waiting=None):
        spins = spins_of(psi)
        send = send_buffer.at[sweep]
        recv = recv_buffer.at[sweep]
        ahead = [project(spins, mu, -1) for mu in range(4)]
        behind = [link_times(links, mu, project(spins, mu, 1), True) for mu in range(4)]

        x_ahead = pack_slots(ahead[3], 3, True, places)
        x_behind = pack_slots(behind[3], 3, False, places)
        send[X_BOTH : X_BOTH + 3] = choose(places.block == 0, x_ahead, x_behind)
        t_ahead, t_ahead_state = pack_time(ahead[0], True, places)
        send[T_AHEAD : T_AHEAD + 3] = t_ahead
        t_behind, t_behind_state = pack_time(behind[0], False, places)
        send[T_BEHIND : T_BEHIND + 3] = t_behind
        send[Y_AHEAD : Y_AHEAD + 3] = pack_slots(ahead[2], 2, True, places)
        send[Y_BEHIND : Y_BEHIND + 3] = pack_slots(behind[2], 2, False, places)
        send[Z_BOTH : Z_BOTH + 3] = pack_slots(ahead[1], 1, True, places)
        send[Z_BOTH + 3 : Z_BOTH + 6] = pack_slots(behind[1], 1, False, places)

        messages = [
            message(sweep, 0, X_BOTH, 3, x_other),
            message(sweep, 1, T_AHEAD, 3, t_prior),
            message(sweep, 2, T_BEHIND, 3, t_next),
            message(sweep, 3, Y_AHEAD, 3, y_prior),
            message(sweep, 4, Y_BEHIND, 3, y_next),
            message(sweep, 5, Z_BOTH, 6, z_other),
        ]
        if before_send is not None:
            before_send()
        for copy in messages:
            copy.start()
            started.append(copy)
        if while_waiting is not None:
            while_waiting()

        ahead_moved = {mu: lane_roll(ahead[mu], -STRIDE[mu]) for mu in (1, 2, 3)}
        behind_moved = {mu: lane_roll(behind[mu], STRIDE[mu]) for mu in (1, 2, 3)}
        zero = jnp.zeros((3, 8, 128), F32)
        summed = [(zero, zero)] * 4

        def finish(summed, mu, from_ahead, from_behind):
            summed = lift(summed, link_times(links, mu, from_ahead, False), mu, -1)
            return lift(summed, from_behind, mu, 1)

        messages[5].wait_recv()
        summed = finish(
            summed,
            1,
            merge_slots(ahead_moved[1], recv[Z_BOTH : Z_BOTH + 3], 1, True, places),
            merge_slots(behind_moved[1], recv[Z_BOTH + 3 : Z_BOTH + 6], 1, False, places),
        )
        messages[3].wait_recv()
        messages[4].wait_recv()
        summed = finish(
            summed,
            2,
            merge_slots(ahead_moved[2], recv[Y_AHEAD : Y_AHEAD + 3], 2, True, places),
            merge_slots(behind_moved[2], recv[Y_BEHIND : Y_BEHIND + 3], 2, False, places),
        )
        messages[1].wait_recv()
        messages[2].wait_recv()
        summed = finish(
            summed,
            0,
            merge_time(t_ahead_state, recv[T_AHEAD : T_AHEAD + 3], True, places),
            merge_time(t_behind_state, recv[T_BEHIND : T_BEHIND + 3], False, places),
        )
        messages[0].wait_recv()
        x_recv = recv[X_BOTH : X_BOTH + 3]
        x_from_ahead = choose(places.block == 3, row_roll(x_recv, 3), row_roll(x_ahead, -1))
        x_from_behind = choose(places.block == 0, row_roll(x_recv, -3), row_roll(x_behind, 1))
        summed = finish(
            summed,
            3,
            merge_slots(ahead_moved[3], x_from_ahead, 3, True, places),
            merge_slots(behind_moved[3], x_from_behind, 3, False, places),
        )

        result = []
        for chirality in range(2):
            pair = summed[2 * chirality : 2 * chirality + 2]
            out_real = out_imag = None
            for column in range(6):
                c_real = clover[chirality, 0, :, column]
                c_imag = clover[chirality, 1, :, column]
                v_real = pair[column // 3][0][column % 3][None]
                v_imag = pair[column // 3][1][column % 3][None]
                term_real = c_real * v_real - c_imag * v_imag
                term_imag = c_real * v_imag + c_imag * v_real
                out_real = term_real if out_real is None else out_real + term_real
                out_imag = term_imag if out_imag is None else out_imag + term_imag
            result.append((out_real[:3], out_imag[:3]))
            result.append((out_real[3:], out_imag[3:]))
        return tiles_of(result)

    loads[0].wait()
    source = source_ref[...]
    scaled[...] = fine_relax * source
    loads[1].wait()
    links[...] = links_raw[...].astype(F32).reshape(links.shape)

    def convert():
        loads[2].wait()
        clover[...] = (fine_relax * kappa_value) * clover_raw[...].astype(F32).reshape(clover.shape)
        loads[3].wait()
        for pair in range(6):
            both = vectors_raw[:, pair].astype(F32).reshape(32, 2, 8, 128)
            for side in range(2):
                place = (2 * pair + side) * 128
                matrix[:, place : place + 128] = both[:, side].reshape(256, 128).astype(BF16)

    def enter():
        pl.semaphore_wait(barrier, 6)

    psi = scaled[...]
    psi = (1.0 - fine_relax) * psi + scaled[...] + clover_hopping(0, psi, enter, convert)

    change = clover_hopping(1, psi)
    residual = source_ref[...] - psi + (1.0 / fine_relax) * change

    stacked = jnp.stack([residual[:12], residual[12:]], axis=1).reshape(12, 16, 128).astype(BF16)
    flat = jnp.concatenate([stacked[c] for c in range(12)], axis=1)
    products = lax.dot_general(
        flat, matrix[...], (((1,), (1,)), ((), ())), preferred_element_type=F32
    )
    wide_row = lax.broadcasted_iota(jnp.int32, (16, 256), 0)
    wide_lane = lax.broadcasted_iota(jnp.int32, (16, 256), 1)
    same_row = wide_row % 8 == wide_lane % 8
    products = jnp.where(same_row, products, 0.0)
    high = products.astype(BF16)
    low = (products - high.astype(F32)).astype(BF16)
    gather_row = lax.broadcasted_iota(jnp.int32, (256, 128), 0)
    gather_lane = lax.broadcasted_iota(jnp.int32, (256, 128), 1)
    gather = (gather_lane == gather_row // 16 + 16 * ((gather_row // 8) % 2)).astype(F32).astype(BF16)
    sums = jnp.dot(high, gather, preferred_element_type=F32) + jnp.dot(
        low, gather, preferred_element_type=F32
    )
    with_real, with_imag = sums[:8], sums[8:]
    narrow = places.lane < 16
    coarse_real = jnp.where(narrow, with_real + lane_roll(with_imag, -16), 0.0)
    coarse_imag = jnp.where(narrow, with_imag - lane_roll(with_real, -16), 0.0)
    coarse_real = coarse_real + row_roll(coarse_real, 4)
    coarse_imag = coarse_imag + row_roll(coarse_imag, 4)

    own = jnp.where(places.half == 0, coarse_real, coarse_imag)
    coarse_send[...] = own
    coarse_messages = []
    for number, target in enumerate((x_other, t_prior, t_next, y_prior, y_next, z_other)):
        copy = pltpu.make_async_remote_copy(
            src_ref=coarse_send,
            dst_ref=coarse_recv.at[number],
            send_sem=coarse_send_sem.at[number],
            recv_sem=coarse_recv_sem.at[number],
            device_id=target,
            device_id_type=pl.DeviceIdType.MESH,
        )
        copy.start()
        coarse_messages.append(copy)
        started.append(copy)
    loads[4].wait()

    accumulated = [jnp.zeros((8, 8, 16), F32), jnp.zeros((8, 8, 16), F32)]

    def add_hop(number, tile):
        tile = coarse_relax * tile
        swapped = row_roll(tile, 4)
        e_real = jnp.where(places.half == 0, tile, swapped)[:, :16][None]
        e_imag = jnp.where(places.half == 0, swapped, tile)[:, :16][None]
        h_real, h_imag = hops_ref[number, 0], hops_ref[number, 1]
        accumulated[0] = accumulated[0] + (h_real * e_real - h_imag * e_imag)
        accumulated[1] = accumulated[1] + (h_real * e_imag + h_imag * e_real)

    coarse_messages[5].wait_recv()
    z_tile = coarse_recv[5]
    add_hop(2, z_tile)
    add_hop(3, z_tile)
    coarse_messages[3].wait_recv()
    add_hop(4, coarse_recv[3])
    coarse_messages[4].wait_recv()
    add_hop(5, coarse_recv[4])
    coarse_messages[1].wait_recv()
    add_hop(0, coarse_recv[1])
    coarse_messages[2].wait_recv()
    add_hop(1, coarse_recv[2])
    coarse_messages[0].wait_recv()
    x_tile = coarse_recv[0]
    add_hop(6, jnp.where(places.block == 3, row_roll(x_tile, 3), row_roll(own, -1)))
    add_hop(7, jnp.where(places.block == 0, row_roll(x_tile, -3), row_roll(own, 1)))

    def gathered(values):
        totals = jnp.sum(values, axis=-1, keepdims=True)
        spread = jnp.zeros((8, 128), F32)
        for pair in range(8):
            column = jnp.broadcast_to(totals[pair], (8, 128))
            spread = jnp.where(places.lane // 2 == pair, column, spread)
        return jnp.where(places.lane % 2 == places.half, spread, row_roll(spread, 4))

    first_real, first_imag = coarse_relax * coarse_real, coarse_relax * coarse_imag
    error_real = first_real + coarse_relax * (
        coarse_real - (first_real - gathered(accumulated[0]))
    )
    error_imag = first_imag + coarse_relax * (
        coarse_imag - (first_imag - gathered(accumulated[1]))
    )
    coarse_ref[0] = error_real[:4, :16]
    coarse_ref[1] = error_imag[:4, :16]

    error_real = jnp.where(narrow, error_real, 0.0)
    error_imag = jnp.where(narrow, error_imag, 0.0)
    weights = jnp.concatenate(
        [error_real - lane_roll(error_imag, 16), error_imag + lane_roll(error_real, 16)], axis=0
    ).astype(BF16)
    scatter_row = lax.broadcasted_iota(jnp.int32, (128, 256), 0)
    scatter_lane = lax.broadcasted_iota(jnp.int32, (128, 256), 1)
    scatter = (
        (scatter_row == scatter_lane // 16 + 16 * ((scatter_lane // 8) % 2)).astype(F32).astype(BF16)
    )
    spread_weights = jnp.dot(weights, scatter, preferred_element_type=F32)
    spread_weights = jnp.where(same_row, spread_weights, 0.0).astype(BF16)
    correction = jnp.dot(spread_weights, matrix[...], preferred_element_type=F32)
    correction = jnp.concatenate(
        [correction[:8, 128 * c : 128 * c + 128][None] for c in range(12)]
        + [correction[8:, 128 * c : 128 * c + 128][None] for c in range(12)],
        axis=0,
    )
    psi = psi + correction

    for sweep in (2, 3):
        psi = (1.0 - fine_relax) * psi + scaled[...] + clover_hopping(sweep, psi)
    out_ref[...] = psi

    for copy in started:
        copy.wait_send()


def rows_of_eight(values):
    count = values.size // 1024
    return values.reshape(count, 4, 2, 128).transpose(0, 2, 1, 3).reshape(count, 8, 128)


def local(source, gauge_links, clover_inverse, vectors, coarse_hops):
    source_tiles = rows_of_eight(source)
    link_tiles = rows_of_eight(gauge_links).reshape(36, 16, 128)
    clover_tiles = rows_of_eight(clover_inverse).reshape(72, 16, 128)
    vector_tiles = rows_of_eight(vectors).reshape(32, 6, 16, 128)
    hop_tiles = (
        coarse_hops.reshape(8, 2, 16, 16, 4).transpose(0, 1, 2, 4, 3).reshape(8, 2, 8, 8, 16)
    )
    out, coarse = pl.pallas_call(
        kernel,
        out_shape=(
            jax.ShapeDtypeStruct((24, 8, 128), F32),
            jax.ShapeDtypeStruct((2, 4, 16), F32),
        ),
        in_specs=[pl.BlockSpec(memory_space=pltpu.HBM)] * 5,
        out_specs=(
            pl.BlockSpec(memory_space=pltpu.VMEM),
            pl.BlockSpec(memory_space=pltpu.VMEM),
        ),
        scratch_shapes=[
            pltpu.VMEM((24, 8, 128), F32),
            pltpu.VMEM((36, 16, 128), BF16),
            pltpu.VMEM((72, 16, 128), BF16),
            pltpu.VMEM((32, 6, 16, 128), BF16),
            pltpu.VMEM((8, 2, 8, 8, 16), F32),
            pltpu.VMEM((4, 2, 3, 3, 8, 128), F32),
            pltpu.VMEM((2, 2, 6, 6, 8, 128), F32),
            pltpu.VMEM((256, 1536), BF16),
            pltpu.VMEM((24, 8, 128), F32),
            pltpu.VMEM((4, TILES, 8, 128), F32),
            pltpu.VMEM((4, TILES, 8, 128), F32),
            pltpu.VMEM((8, 128), F32),
            pltpu.VMEM((6, 8, 128), F32),
            pltpu.SemaphoreType.DMA((5,)),
            pltpu.SemaphoreType.DMA((4, 6)),
            pltpu.SemaphoreType.DMA((4, 6)),
            pltpu.SemaphoreType.DMA((6,)),
            pltpu.SemaphoreType.DMA((6,)),
        ],
        compiler_params=pltpu.CompilerParams(
            collective_id=0, has_side_effects=True, vmem_limit_bytes=48 * 1024 * 1024
        ),
    )(source_tiles, link_tiles, clover_tiles, vector_tiles, hop_tiles)
    solution_out = (
        out.reshape(24, 2, 4, 128).transpose(0, 2, 1, 3).reshape(2, 4, 3, 1, 1, 1, 4, 256)
    )
    coarse_out = coarse.transpose(0, 2, 1).reshape(2, 16, 1, 1, 1, 4)
    return solution_out, coarse_out


def solution(mesh):
    return jax.shard_map(
        local,
        mesh=mesh,
        in_specs=(
            P(None, None, None, "ta", "gz", "gy", "gx", None),
            P(None, None, None, None, "ta", "gz", "gy", "gx", None),
            P(None, None, None, None, "ta", "gz", "gy", "gx", None),
            P(None, None, None, None, "ta", "gz", "gy", "gx", None),
            P(None, None, None, None, "ta", "gz", "gy", "gx"),
        ),
        out_specs=(
            P(None, None, None, "ta", "gz", "gy", "gx", None),
            P(None, None, "ta", "gz", "gy", "gx"),
        ),
        check_vma=False,
    )
```

```python
import jax
import jax.numpy as jnp
from jax import lax
from jax.experimental import pallas as pl
from jax.experimental.pallas import tpu as pltpu
from jax.sharding import PartitionSpec as P


kappa_value = 0.125
fine_relax = 0.8
coarse_relax = 0.7

F32 = jnp.float32
BF16 = jnp.bfloat16

B_ROWS = (((0, 0), (1, 0)), ((0, 3), (1, 1)), ((1, 2), (0, 0)), ((1, 3), (0, 3)))
B_ADJOINT_ROWS = (((0, 0), (1, 0)), ((0, 1), (1, 3)), ((1, 0), (0, 2)), ((1, 1), (0, 1)))

T_AHEAD, T_BEHIND, Y_AHEAD, Y_BEHIND, Z_BOTH, X_BOTH = 0, 3, 6, 9, 12, 18
TILES = 21


def plus_unit(target, unit, value):
    if unit == 0:
        return target[0] + value[0], target[1] + value[1]
    if unit == 1:
        return target[0] - value[1], target[1] + value[0]
    if unit == 2:
        return target[0] - value[0], target[1] - value[1]
    return target[0] + value[1], target[1] - value[0]


def project(spins, direction, sign):
    halves = []
    for row in range(2):
        column, unit = B_ROWS[direction][row]
        unit = unit if sign > 0 else (unit + 2) % 4
        halves.append(plus_unit(spins[row], unit, spins[2 + column]))
    return jnp.concatenate([halves[0][0], halves[1][0], halves[0][1], halves[1][1]], axis=0)


def lift(summed, half, direction, sign):
    pair = [(half[0:3], half[6:9]), (half[3:6], half[9:12])]
    result = []
    for row in range(2):
        result.append(plus_unit(summed[row], 0, pair[row]))
    for row in range(2):
        column, unit = B_ADJOINT_ROWS[direction][row]
        unit = unit if sign > 0 else (unit + 2) % 4
        result.append(plus_unit(summed[2 + row], unit, pair[column]))
    return result


def link_times(links, direction, half, dagger):
    real_part = half[:6].reshape(2, 3, 8, 128)
    imag_part = half[6:].reshape(2, 3, 8, 128)
    out_real = out_imag = None
    for b in range(3):
        if dagger:
            u_real, u_imag = links[direction, 0, b], links[direction, 1, b]
        else:
            u_real, u_imag = links[direction, 0, :, b], links[direction, 1, :, b]
        u_real, u_imag = u_real[None], u_imag[None]
        v_real, v_imag = real_part[:, b][:, None], imag_part[:, b][:, None]
        if dagger:
            term_real = u_real * v_real + u_imag * v_imag
            term_imag = u_real * v_imag - u_imag * v_real
        else:
            term_real = u_real * v_real - u_imag * v_imag
            term_imag = u_real * v_imag + u_imag * v_real
        out_real = term_real if out_real is None else out_real + term_real
        out_imag = term_imag if out_imag is None else out_imag + term_imag
    return jnp.concatenate([out_real.reshape(6, 8, 128), out_imag.reshape(6, 8, 128)], axis=0)


def lane_roll(values, shift):
    shift = shift % 128
    return values if shift == 0 else pltpu.roll(values, shift, values.ndim - 1)


def row_roll(values, shift):
    shift = shift % 8
    return values if shift == 0 else pltpu.roll(values, shift, values.ndim - 2)


class Places:
    def __init__(self):
        row = lax.broadcasted_iota(jnp.int32, (8, 128), 0)
        lane = lax.broadcasted_iota(jnp.int32, (8, 128), 1)
        self.row, self.lane = row, lane
        self.block = row % 4
        self.half = row // 4
        self.parity = lane // 64
        self.slot = {1: (lane // 16) % 4, 2: (lane // 4) % 4, 3: lane % 4}


STRIDE = {1: 16, 2: 4, 3: 1}


def choose(mask, first, second):
    return jnp.where(jnp.broadcast_to(mask[None], first.shape), first, second)


def pack_slots(half, direction, ahead, places):
    stride, slot = STRIDE[direction], places.slot[direction]
    fours = half.reshape(3, 4, 8, 128)
    packed = fours[:, 0]
    for k in range(1, 4):
        if ahead:
            packed = choose(slot == k, lane_roll(fours[:, k], stride * k), packed)
        else:
            packed = choose(slot == 3 - k, lane_roll(fours[:, k], -stride * k), packed)
    return packed


def merge_slots(rolled, packed, direction, ahead, places):
    stride, slot = STRIDE[direction], places.slot[direction]
    fours = rolled.reshape(3, 4, 8, 128)
    merged = []
    for k in range(4):
        if ahead:
            merged.append(choose(slot == 3, lane_roll(packed, stride * (3 - k)), fours[:, k]))
        else:
            merged.append(choose(slot == 0, lane_roll(packed, -stride * (3 - k)), fours[:, k]))
    return jnp.stack(merged, axis=1).reshape(12, 8, 128)


def pack_time(half, ahead, places):
    edge = places.parity == (0 if ahead else 1)
    edge_rows = places.half == (0 if ahead else 1)
    pairs = half.reshape(6, 2, 8, 128)
    first, second = pairs[:, 0], lane_roll(pairs[:, 1], 64)
    paired = choose(edge, first, second).reshape(3, 2, 8, 128)
    paired_first, paired_second = paired[:, 0], row_roll(paired[:, 1], 4)
    packed = choose(edge_rows, paired_first, paired_second)
    return packed, (first, second, paired_first, paired_second)


def merge_time(state, packed, ahead, places):
    edge = places.parity == (0 if ahead else 1)
    edge_rows = places.half == (0 if ahead else 1)
    first, second, paired_first, paired_second = state
    next_first = row_roll(choose(edge_rows, packed, paired_first), 4)
    next_second = choose(edge_rows, paired_second, packed)
    moved = jnp.stack([next_first, next_second], axis=1).reshape(6, 8, 128)
    out_first = lane_roll(choose(edge, moved, first), 64)
    out_second = choose(edge, second, moved)
    return jnp.stack([out_first, out_second], axis=1).reshape(12, 8, 128)


def spins_of(values):
    return [(values[3 * s : 3 * s + 3], values[12 + 3 * s : 15 + 3 * s]) for s in range(4)]


def tiles_of(spins):
    return jnp.concatenate([spin[0] for spin in spins] + [spin[1] for spin in spins], axis=0)


def kernel(
    source_hbm,
    links_hbm,
    clover_hbm,
    vectors_hbm,
    hops_hbm,
    out_ref,
    coarse_ref,
    source_ref,
    links_raw,
    clover_raw,
    vectors_raw,
    hops_ref,
    links,
    clover,
    matrix,
    scaled,
    send_buffer,
    recv_buffer,
    coarse_send,
    coarse_recv,
    load_sem,
    send_sem,
    recv_sem,
    coarse_send_sem,
    coarse_recv_sem,
):
    loads = []
    for index, (origin, target) in enumerate(
        (
            (source_hbm, source_ref),
            (links_hbm, links_raw),
            (clover_hbm, clover_raw),
            (vectors_hbm, vectors_raw),
            (hops_hbm, hops_ref),
        )
    ):
        loads.append(pltpu.make_async_copy(origin, target, load_sem.at[index]))
    loads[0].start()
    loads[1].start()

    def around(axis, step):
        count = lax.axis_size(axis)
        return {axis: lax.rem(lax.axis_index(axis) + (step + count), count)}

    t_next, t_prior = around("ta", 1), around("ta", -1)
    y_next, y_prior = around("gy", 1), around("gy", -1)
    z_other, x_other = around("gz", 1), around("gx", 1)

    barrier = pltpu.get_barrier_semaphore()
    for neighbour in (t_next, t_prior, y_next, y_prior, z_other, x_other):
        pl.semaphore_signal(
            barrier, inc=1, device_id=neighbour, device_id_type=pl.DeviceIdType.MESH
        )

    places = Places()

    def message(sweep, number, start, count, target):
        window = pl.ds(start, count)
        return pltpu.make_async_remote_copy(
            src_ref=send_buffer.at[sweep, window],
            dst_ref=recv_buffer.at[sweep, window],
            send_sem=send_sem.at[sweep, number],
            recv_sem=recv_sem.at[sweep, number],
            device_id=target,
            device_id_type=pl.DeviceIdType.MESH,
        )

    started = []

    def clover_hopping(sweep, psi, before_send=None, while_waiting=None):
        spins = spins_of(psi)
        send = send_buffer.at[sweep]
        recv = recv_buffer.at[sweep]
        ahead, behind, messages = {}, {}, {}

        def halves(mu):
            ahead[mu] = project(spins, mu, -1)
            behind[mu] = link_times(links, mu, project(spins, mu, 1), True)

        def dispatch(number, start, count, target):
            messages[number] = message(sweep, number, start, count, target)
            messages[number].start()
            started.append(messages[number])

        ahead[0] = project(spins, 0, -1)
        t_ahead, t_ahead_state = pack_time(ahead[0], True, places)
        send[T_AHEAD : T_AHEAD + 3] = t_ahead
        if before_send is not None:
            before_send()
        dispatch(1, T_AHEAD, 3, t_prior)
        behind[0] = link_times(links, 0, project(spins, 0, 1), True)
        t_behind, t_behind_state = pack_time(behind[0], False, places)
        send[T_BEHIND : T_BEHIND + 3] = t_behind
        dispatch(2, T_BEHIND, 3, t_next)
        halves(3)
        x_ahead = pack_slots(ahead[3], 3, True, places)
        x_behind = pack_slots(behind[3], 3, False, places)
        send[X_BOTH : X_BOTH + 3] = choose(places.block == 0, x_ahead, x_behind)
        dispatch(0, X_BOTH, 3, x_other)
        halves(2)
        send[Y_AHEAD : Y_AHEAD + 3] = pack_slots(ahead[2], 2, True, places)
        dispatch(3, Y_AHEAD, 3, y_prior)
        send[Y_BEHIND : Y_BEHIND + 3] = pack_slots(behind[2], 2, False, places)
        dispatch(4, Y_BEHIND, 3, y_next)
        halves(1)
        send[Z_BOTH : Z_BOTH + 3] = pack_slots(ahead[1], 1, True, places)
        send[Z_BOTH + 3 : Z_BOTH + 6] = pack_slots(behind[1], 1, False, places)
        dispatch(5, Z_BOTH, 6, z_other)
        if while_waiting is not None:
            while_waiting()

        ahead_moved = {mu: lane_roll(ahead[mu], -STRIDE[mu]) for mu in (1, 2, 3)}
        behind_moved = {mu: lane_roll(behind[mu], STRIDE[mu]) for mu in (1, 2, 3)}
        zero = jnp.zeros((3, 8, 128), F32)
        summed = [(zero, zero)] * 4

        def finish(summed, mu, from_ahead, from_behind):
            summed = lift(summed, link_times(links, mu, from_ahead, False), mu, -1)
            return lift(summed, from_behind, mu, 1)

        messages[5].wait_recv()
        summed = finish(
            summed,
            1,
            merge_slots(ahead_moved[1], recv[Z_BOTH : Z_BOTH + 3], 1, True, places),
            merge_slots(behind_moved[1], recv[Z_BOTH + 3 : Z_BOTH + 6], 1, False, places),
        )
        messages[3].wait_recv()
        messages[4].wait_recv()
        summed = finish(
            summed,
            2,
            merge_slots(ahead_moved[2], recv[Y_AHEAD : Y_AHEAD + 3], 2, True, places),
            merge_slots(behind_moved[2], recv[Y_BEHIND : Y_BEHIND + 3], 2, False, places),
        )
        messages[0].wait_recv()
        x_recv = recv[X_BOTH : X_BOTH + 3]
        x_from_ahead = choose(places.block == 3, row_roll(x_recv, 3), row_roll(x_ahead, -1))
        x_from_behind = choose(places.block == 0, row_roll(x_recv, -3), row_roll(x_behind, 1))
        summed = finish(
            summed,
            3,
            merge_slots(ahead_moved[3], x_from_ahead, 3, True, places),
            merge_slots(behind_moved[3], x_from_behind, 3, False, places),
        )
        messages[1].wait_recv()
        messages[2].wait_recv()
        summed = finish(
            summed,
            0,
            merge_time(t_ahead_state, recv[T_AHEAD : T_AHEAD + 3], True, places),
            merge_time(t_behind_state, recv[T_BEHIND : T_BEHIND + 3], False, places),
        )

        result = []
        for chirality in range(2):
            pair = summed[2 * chirality : 2 * chirality + 2]
            out_real = out_imag = None
            for column in range(6):
                c_real = clover[chirality, 0, :, column]
                c_imag = clover[chirality, 1, :, column]
                v_real = pair[column // 3][0][column % 3][None]
                v_imag = pair[column // 3][1][column % 3][None]
                term_real = c_real * v_real - c_imag * v_imag
                term_imag = c_real * v_imag + c_imag * v_real
                out_real = term_real if out_real is None else out_real + term_real
                out_imag = term_imag if out_imag is None else out_imag + term_imag
            result.append((out_real[:3], out_imag[:3]))
            result.append((out_real[3:], out_imag[3:]))
        return tiles_of(result)

    loads[0].wait()
    scaled[...] = fine_relax * source_ref[...]

    def convert():
        loads[2].wait()
        clover[...] = (fine_relax * kappa_value) * clover_raw[...].astype(F32).reshape(clover.shape)
        loads[3].wait()
        for pair in range(6):
            both = vectors_raw[:, pair].astype(F32).reshape(32, 2, 8, 128)
            for side in range(2):
                place = (2 * pair + side) * 128
                matrix[:, place : place + 128] = both[:, side].reshape(256, 128).astype(BF16)

    def enter():
        loads[1].wait()
        for load in loads[2:]:
            load.start()
        links[...] = links_raw[...].astype(F32).reshape(links.shape)
        pl.semaphore_wait(barrier, 6)

    psi = scaled[...]
    psi = (1.0 - fine_relax) * psi + scaled[...] + clover_hopping(0, psi, enter, convert)

    change = clover_hopping(1, psi)
    residual = source_ref[...] - psi + (1.0 / fine_relax) * change

    stacked = jnp.stack([residual[:12], residual[12:]], axis=1).reshape(12, 16, 128).astype(BF16)
    flat = jnp.concatenate([stacked[c] for c in range(12)], axis=1)
    products = lax.dot_general(
        flat, matrix[...], (((1,), (1,)), ((), ())), preferred_element_type=F32
    )
    wide_row = lax.broadcasted_iota(jnp.int32, (16, 256), 0)
    wide_lane = lax.broadcasted_iota(jnp.int32, (16, 256), 1)
    same_row = wide_row % 8 == wide_lane % 8
    products = jnp.where(same_row, products, 0.0)
    high = products.astype(BF16)
    low = (products - high.astype(F32)).astype(BF16)
    gather_row = lax.broadcasted_iota(jnp.int32, (256, 128), 0)
    gather_lane = lax.broadcasted_iota(jnp.int32, (256, 128), 1)
    gather = (gather_lane == gather_row // 16 + 16 * ((gather_row // 8) % 2)).astype(F32).astype(BF16)
    sums = jnp.dot(high, gather, preferred_element_type=F32) + jnp.dot(
        low, gather, preferred_element_type=F32
    )
    with_real, with_imag = sums[:8], sums[8:]
    narrow = places.lane < 16
    coarse_real = jnp.where(narrow, with_real + lane_roll(with_imag, -16), 0.0)
    coarse_imag = jnp.where(narrow, with_imag - lane_roll(with_real, -16), 0.0)
    coarse_real = coarse_real + row_roll(coarse_real, 4)
    coarse_imag = coarse_imag + row_roll(coarse_imag, 4)

    own = jnp.where(places.half == 0, coarse_real, coarse_imag)
    coarse_send[...] = own
    coarse_messages = {}
    for number, target in ((1, t_prior), (2, t_next), (0, x_other), (3, y_prior), (4, y_next), (5, z_other)):
        copy = pltpu.make_async_remote_copy(
            src_ref=coarse_send,
            dst_ref=coarse_recv.at[number],
            send_sem=coarse_send_sem.at[number],
            recv_sem=coarse_recv_sem.at[number],
            device_id=target,
            device_id_type=pl.DeviceIdType.MESH,
        )
        copy.start()
        coarse_messages[number] = copy
        started.append(copy)
    loads[4].wait()

    accumulated = [jnp.zeros((8, 8, 16), F32), jnp.zeros((8, 8, 16), F32)]

    def add_hop(number, tile):
        tile = coarse_relax * tile
        swapped = row_roll(tile, 4)
        e_real = jnp.where(places.half == 0, tile, swapped)[:, :16][None]
        e_imag = jnp.where(places.half == 0, swapped, tile)[:, :16][None]
        h_real, h_imag = hops_ref[number, 0], hops_ref[number, 1]
        accumulated[0] = accumulated[0] + (h_real * e_real - h_imag * e_imag)
        accumulated[1] = accumulated[1] + (h_real * e_imag + h_imag * e_real)

    coarse_messages[5].wait_recv()
    z_tile = coarse_recv[5]
    add_hop(2, z_tile)
    add_hop(3, z_tile)
    coarse_messages[3].wait_recv()
    add_hop(4, coarse_recv[3])
    coarse_messages[4].wait_recv()
    add_hop(5, coarse_recv[4])
    coarse_messages[0].wait_recv()
    x_tile = coarse_recv[0]
    add_hop(6, jnp.where(places.block == 3, row_roll(x_tile, 3), row_roll(own, -1)))
    add_hop(7, jnp.where(places.block == 0, row_roll(x_tile, -3), row_roll(own, 1)))
    coarse_messages[1].wait_recv()
    add_hop(0, coarse_recv[1])
    coarse_messages[2].wait_recv()
    add_hop(1, coarse_recv[2])

    def gathered(values):
        totals = jnp.sum(values, axis=-1, keepdims=True)
        spread = jnp.zeros((8, 128), F32)
        for pair in range(8):
            column = jnp.broadcast_to(totals[pair], (8, 128))
            spread = jnp.where(places.lane // 2 == pair, column, spread)
        return jnp.where(places.lane % 2 == places.half, spread, row_roll(spread, 4))

    first_real, first_imag = coarse_relax * coarse_real, coarse_relax * coarse_imag
    error_real = first_real + coarse_relax * (
        coarse_real - (first_real - gathered(accumulated[0]))
    )
    error_imag = first_imag + coarse_relax * (
        coarse_imag - (first_imag - gathered(accumulated[1]))
    )
    coarse_ref[0] = error_real[:4, :16]
    coarse_ref[1] = error_imag[:4, :16]

    error_real = jnp.where(narrow, error_real, 0.0)
    error_imag = jnp.where(narrow, error_imag, 0.0)
    weights = jnp.concatenate(
        [error_real - lane_roll(error_imag, 16), error_imag + lane_roll(error_real, 16)], axis=0
    ).astype(BF16)
    scatter_row = lax.broadcasted_iota(jnp.int32, (128, 256), 0)
    scatter_lane = lax.broadcasted_iota(jnp.int32, (128, 256), 1)
    scatter = (
        (scatter_row == scatter_lane // 16 + 16 * ((scatter_lane // 8) % 2)).astype(F32).astype(BF16)
    )
    spread_weights = jnp.dot(weights, scatter, preferred_element_type=F32)
    spread_weights = jnp.where(same_row, spread_weights, 0.0).astype(BF16)
    correction = jnp.dot(spread_weights, matrix[...], preferred_element_type=F32)
    correction = jnp.concatenate(
        [correction[:8, 128 * c : 128 * c + 128][None] for c in range(12)]
        + [correction[8:, 128 * c : 128 * c + 128][None] for c in range(12)],
        axis=0,
    )
    psi = psi + correction

    for sweep in (2, 3):
        psi = (1.0 - fine_relax) * psi + scaled[...] + clover_hopping(sweep, psi)
    out_ref[...] = psi

    for copy in started:
        copy.wait_send()


def deliver(out_in, coarse_in, out_ref, coarse_ref, sems):
    copies = [
        pltpu.make_async_copy(out_in, out_ref, sems.at[0]),
        pltpu.make_async_copy(coarse_in, coarse_ref, sems.at[1]),
    ]
    for copy in copies:
        copy.start()
    for copy in copies:
        copy.wait()


def rows_of_eight(values):
    count = values.size // 1024
    return values.reshape(count, 4, 2, 128).transpose(0, 2, 1, 3).reshape(count, 8, 128)


def local(source, gauge_links, clover_inverse, vectors, coarse_hops):
    source_tiles = rows_of_eight(source)
    link_tiles = rows_of_eight(gauge_links).reshape(36, 16, 128)
    clover_tiles = rows_of_eight(clover_inverse).reshape(72, 16, 128)
    vector_tiles = rows_of_eight(vectors).reshape(32, 6, 16, 128)
    hop_tiles = (
        coarse_hops.reshape(8, 2, 16, 16, 4).transpose(0, 1, 2, 4, 3).reshape(8, 2, 8, 8, 16)
    )
    out, coarse = pl.pallas_call(
        kernel,
        out_shape=(
            jax.ShapeDtypeStruct((24, 8, 128), F32),
            jax.ShapeDtypeStruct((2, 4, 16), F32),
        ),
        in_specs=[pl.BlockSpec(memory_space=pltpu.HBM)] * 5,
        out_specs=(
            pl.BlockSpec(memory_space=pltpu.VMEM),
            pl.BlockSpec(memory_space=pltpu.VMEM),
        ),
        scratch_shapes=[
            pltpu.VMEM((24, 8, 128), F32),
            pltpu.VMEM((36, 16, 128), BF16),
            pltpu.VMEM((72, 16, 128), BF16),
            pltpu.VMEM((32, 6, 16, 128), BF16),
            pltpu.VMEM((8, 2, 8, 8, 16), F32),
            pltpu.VMEM((4, 2, 3, 3, 8, 128), F32),
            pltpu.VMEM((2, 2, 6, 6, 8, 128), F32),
            pltpu.VMEM((256, 1536), BF16),
            pltpu.VMEM((24, 8, 128), F32),
            pltpu.VMEM((4, TILES, 8, 128), F32),
            pltpu.VMEM((4, TILES, 8, 128), F32),
            pltpu.VMEM((8, 128), F32),
            pltpu.VMEM((6, 8, 128), F32),
            pltpu.SemaphoreType.DMA((5,)),
            pltpu.SemaphoreType.DMA((4, 6)),
            pltpu.SemaphoreType.DMA((4, 6)),
            pltpu.SemaphoreType.DMA((6,)),
            pltpu.SemaphoreType.DMA((6,)),
        ],
        compiler_params=pltpu.CompilerParams(
            collective_id=0, has_side_effects=True, vmem_limit_bytes=55040 * 1024
        ),
    )(source_tiles, link_tiles, clover_tiles, vector_tiles, hop_tiles)
    out, coarse = pl.pallas_call(
        deliver,
        out_shape=(
            jax.ShapeDtypeStruct((24, 8, 128), F32),
            jax.ShapeDtypeStruct((2, 4, 16), F32),
        ),
        in_specs=[pl.BlockSpec(memory_space=pl.ANY)] * 2,
        out_specs=[pl.BlockSpec(memory_space=pl.ANY)] * 2,
        scratch_shapes=[pltpu.SemaphoreType.DMA((2,))],
        compiler_params=pltpu.CompilerParams(vmem_limit_bytes=1024 * 1024),
    )(out, coarse)
    solution_out = (
        out.reshape(24, 2, 4, 128).transpose(0, 2, 1, 3).reshape(2, 4, 3, 1, 1, 1, 4, 256)
    )
    coarse_out = coarse.transpose(0, 2, 1).reshape(2, 16, 1, 1, 1, 4)
    return solution_out, coarse_out


def solution(mesh):
    return jax.shard_map(
        local,
        mesh=mesh,
        in_specs=(
            P(None, None, None, "ta", "gz", "gy", "gx", None),
            P(None, None, None, None, "ta", "gz", "gy", "gx", None),
            P(None, None, None, None, "ta", "gz", "gy", "gx", None),
            P(None, None, None, None, "ta", "gz", "gy", "gx", None),
            P(None, None, None, None, "ta", "gz", "gy", "gx"),
        ),
        out_specs=(
            P(None, None, None, "ta", "gz", "gy", "gx", None),
            P(None, None, "ta", "gz", "gy", "gx"),
        ),
        check_vma=False,
    )
```

```python
import jax
import jax.numpy as jnp
from jax import lax
from jax.experimental import pallas as pl
from jax.experimental.pallas import tpu as pltpu
from jax.sharding import PartitionSpec as P


kappa_value = 0.125
fine_relax = 0.8
coarse_relax = 0.7

F32 = jnp.float32
BF16 = jnp.bfloat16

B_ROWS = (((0, 0), (1, 0)), ((0, 3), (1, 1)), ((1, 2), (0, 0)), ((1, 3), (0, 3)))
B_ADJOINT_ROWS = (((0, 0), (1, 0)), ((0, 1), (1, 3)), ((1, 0), (0, 2)), ((1, 1), (0, 1)))

T_AHEAD, T_BEHIND, Y_AHEAD, Y_BEHIND, Z_BOTH, X_BOTH = 0, 3, 6, 9, 12, 18
TILES = 21


def plus_unit(target, unit, value):
    if unit == 0:
        return target[0] + value[0], target[1] + value[1]
    if unit == 1:
        return target[0] - value[1], target[1] + value[0]
    if unit == 2:
        return target[0] - value[0], target[1] - value[1]
    return target[0] + value[1], target[1] - value[0]


def project(spins, direction, sign):
    halves = []
    for row in range(2):
        column, unit = B_ROWS[direction][row]
        unit = unit if sign > 0 else (unit + 2) % 4
        halves.append(plus_unit(spins[row], unit, spins[2 + column]))
    return jnp.concatenate([halves[0][0], halves[1][0], halves[0][1], halves[1][1]], axis=0)


def lift(summed, half, direction, sign):
    pair = [(half[0:3], half[6:9]), (half[3:6], half[9:12])]
    result = []
    for row in range(2):
        result.append(plus_unit(summed[row], 0, pair[row]))
    for row in range(2):
        column, unit = B_ADJOINT_ROWS[direction][row]
        unit = unit if sign > 0 else (unit + 2) % 4
        result.append(plus_unit(summed[2 + row], unit, pair[column]))
    return result


def link_times(links, direction, half, dagger):
    real_part = half[:6].reshape(2, 3, 8, 128)
    imag_part = half[6:].reshape(2, 3, 8, 128)
    out_real = out_imag = None
    for b in range(3):
        if dagger:
            u_real, u_imag = links[direction, 0, b], links[direction, 1, b]
        else:
            u_real, u_imag = links[direction, 0, :, b], links[direction, 1, :, b]
        u_real, u_imag = u_real[None], u_imag[None]
        v_real, v_imag = real_part[:, b][:, None], imag_part[:, b][:, None]
        if dagger:
            term_real = u_real * v_real + u_imag * v_imag
            term_imag = u_real * v_imag - u_imag * v_real
        else:
            term_real = u_real * v_real - u_imag * v_imag
            term_imag = u_real * v_imag + u_imag * v_real
        out_real = term_real if out_real is None else out_real + term_real
        out_imag = term_imag if out_imag is None else out_imag + term_imag
    return jnp.concatenate([out_real.reshape(6, 8, 128), out_imag.reshape(6, 8, 128)], axis=0)


def lane_roll(values, shift):
    shift = shift % 128
    return values if shift == 0 else pltpu.roll(values, shift, values.ndim - 1)


def row_roll(values, shift):
    shift = shift % 8
    return values if shift == 0 else pltpu.roll(values, shift, values.ndim - 2)


class Places:
    def __init__(self):
        row = lax.broadcasted_iota(jnp.int32, (8, 128), 0)
        lane = lax.broadcasted_iota(jnp.int32, (8, 128), 1)
        self.row, self.lane = row, lane
        self.block = row % 4
        self.half = row // 4
        self.parity = lane // 64
        self.slot = {1: (lane // 16) % 4, 2: (lane // 4) % 4, 3: lane % 4}


STRIDE = {1: 16, 2: 4, 3: 1}


def choose(mask, first, second):
    return jnp.where(jnp.broadcast_to(mask[None], first.shape), first, second)


def pack_slots(half, direction, ahead, places):
    stride, slot = STRIDE[direction], places.slot[direction]
    fours = half.reshape(3, 4, 8, 128)
    packed = fours[:, 0]
    for k in range(1, 4):
        if ahead:
            packed = choose(slot == k, lane_roll(fours[:, k], stride * k), packed)
        else:
            packed = choose(slot == 3 - k, lane_roll(fours[:, k], -stride * k), packed)
    return packed


def merge_slots(rolled, packed, direction, ahead, places):
    stride, slot = STRIDE[direction], places.slot[direction]
    fours = rolled.reshape(3, 4, 8, 128)
    merged = []
    for k in range(4):
        if ahead:
            merged.append(choose(slot == 3, lane_roll(packed, stride * (3 - k)), fours[:, k]))
        else:
            merged.append(choose(slot == 0, lane_roll(packed, -stride * (3 - k)), fours[:, k]))
    return jnp.stack(merged, axis=1).reshape(12, 8, 128)


def pack_time(half, ahead, places):
    edge = places.parity == (0 if ahead else 1)
    edge_rows = places.half == (0 if ahead else 1)
    pairs = half.reshape(6, 2, 8, 128)
    first, second = pairs[:, 0], lane_roll(pairs[:, 1], 64)
    paired = choose(edge, first, second).reshape(3, 2, 8, 128)
    paired_first, paired_second = paired[:, 0], row_roll(paired[:, 1], 4)
    packed = choose(edge_rows, paired_first, paired_second)
    return packed, (first, second, paired_first, paired_second)


def merge_time(state, packed, ahead, places):
    edge = places.parity == (0 if ahead else 1)
    edge_rows = places.half == (0 if ahead else 1)
    first, second, paired_first, paired_second = state
    next_first = row_roll(choose(edge_rows, packed, paired_first), 4)
    next_second = choose(edge_rows, paired_second, packed)
    moved = jnp.stack([next_first, next_second], axis=1).reshape(6, 8, 128)
    out_first = lane_roll(choose(edge, moved, first), 64)
    out_second = choose(edge, second, moved)
    return jnp.stack([out_first, out_second], axis=1).reshape(12, 8, 128)


def spins_of(values):
    return [(values[3 * s : 3 * s + 3], values[12 + 3 * s : 15 + 3 * s]) for s in range(4)]


def tiles_of(spins):
    return jnp.concatenate([spin[0] for spin in spins] + [spin[1] for spin in spins], axis=0)


def kernel(
    source_hbm,
    links_hbm,
    clover_hbm,
    vectors_hbm,
    hops_hbm,
    out_ref,
    coarse_ref,
    source_ref,
    links_raw,
    clover_raw,
    vectors_raw,
    hops_ref,
    links,
    clover,
    matrix,
    matrix_turned,
    gather,
    scatter,
    same_row,
    scaled,
    send_buffer,
    recv_buffer,
    coarse_send,
    coarse_recv,
    load_sem,
    send_sem,
    recv_sem,
    coarse_send_sem,
    coarse_recv_sem,
):
    loads = []
    for index, (origin, target) in enumerate(
        (
            (source_hbm, source_ref),
            (links_hbm, links_raw),
            (clover_hbm, clover_raw),
            (vectors_hbm, vectors_raw),
            (hops_hbm, hops_ref),
        )
    ):
        loads.append(pltpu.make_async_copy(origin, target, load_sem.at[index]))
    loads[0].start()
    loads[1].start()

    def around(axis, step):
        count = lax.axis_size(axis)
        return {axis: lax.rem(lax.axis_index(axis) + (step + count), count)}

    t_next, t_prior = around("ta", 1), around("ta", -1)
    y_next, y_prior = around("gy", 1), around("gy", -1)
    z_other, x_other = around("gz", 1), around("gx", 1)

    barrier = pltpu.get_barrier_semaphore()
    for neighbour in (t_next, t_prior, y_next, y_prior, z_other, x_other):
        pl.semaphore_signal(
            barrier, inc=1, device_id=neighbour, device_id_type=pl.DeviceIdType.MESH
        )

    places = Places()

    def message(sweep, number, start, count, target):
        window = pl.ds(start, count)
        return pltpu.make_async_remote_copy(
            src_ref=send_buffer.at[sweep, window],
            dst_ref=recv_buffer.at[sweep, window],
            send_sem=send_sem.at[sweep, number],
            recv_sem=recv_sem.at[sweep, number],
            device_id=target,
            device_id_type=pl.DeviceIdType.MESH,
        )

    started = []

    def settle(keep):
        while len(started) > keep:
            started.pop(0).wait_send()

    def clover_hopping(sweep, psi, before_send=None, while_waiting=None):
        spins = spins_of(psi)
        send = send_buffer.at[sweep]
        recv = recv_buffer.at[sweep]
        ahead, behind, messages = {}, {}, {}

        def halves(mu):
            ahead[mu] = project(spins, mu, -1)
            behind[mu] = link_times(links, mu, project(spins, mu, 1), True)

        def dispatch(number, start, count, target):
            messages[number] = message(sweep, number, start, count, target)
            messages[number].start()
            started.append(messages[number])

        ahead[0] = project(spins, 0, -1)
        t_ahead, t_ahead_state = pack_time(ahead[0], True, places)
        send[T_AHEAD : T_AHEAD + 3] = t_ahead
        if before_send is not None:
            before_send()
        dispatch(1, T_AHEAD, 3, t_prior)
        behind[0] = link_times(links, 0, project(spins, 0, 1), True)
        t_behind, t_behind_state = pack_time(behind[0], False, places)
        send[T_BEHIND : T_BEHIND + 3] = t_behind
        dispatch(2, T_BEHIND, 3, t_next)
        halves(3)
        x_ahead = pack_slots(ahead[3], 3, True, places)
        x_behind = pack_slots(behind[3], 3, False, places)
        send[X_BOTH : X_BOTH + 3] = choose(places.block == 0, x_ahead, x_behind)
        dispatch(0, X_BOTH, 3, x_other)
        halves(2)
        send[Y_AHEAD : Y_AHEAD + 3] = pack_slots(ahead[2], 2, True, places)
        dispatch(3, Y_AHEAD, 3, y_prior)
        send[Y_BEHIND : Y_BEHIND + 3] = pack_slots(behind[2], 2, False, places)
        dispatch(4, Y_BEHIND, 3, y_next)
        halves(1)
        send[Z_BOTH : Z_BOTH + 3] = pack_slots(ahead[1], 1, True, places)
        send[Z_BOTH + 3 : Z_BOTH + 6] = pack_slots(behind[1], 1, False, places)
        dispatch(5, Z_BOTH, 6, z_other)
        settle(6)
        if while_waiting is not None:
            while_waiting()

        ahead_moved = {mu: lane_roll(ahead[mu], -STRIDE[mu]) for mu in (1, 2, 3)}
        behind_moved = {mu: lane_roll(behind[mu], STRIDE[mu]) for mu in (1, 2, 3)}
        zero = jnp.zeros((3, 8, 128), F32)
        summed = [(zero, zero)] * 4

        def finish(summed, mu, from_ahead, from_behind):
            summed = lift(summed, link_times(links, mu, from_ahead, False), mu, -1)
            return lift(summed, from_behind, mu, 1)

        messages[5].wait_recv()
        summed = finish(
            summed,
            1,
            merge_slots(ahead_moved[1], recv[Z_BOTH : Z_BOTH + 3], 1, True, places),
            merge_slots(behind_moved[1], recv[Z_BOTH + 3 : Z_BOTH + 6], 1, False, places),
        )
        messages[3].wait_recv()
        messages[4].wait_recv()
        summed = finish(
            summed,
            2,
            merge_slots(ahead_moved[2], recv[Y_AHEAD : Y_AHEAD + 3], 2, True, places),
            merge_slots(behind_moved[2], recv[Y_BEHIND : Y_BEHIND + 3], 2, False, places),
        )
        messages[0].wait_recv()
        x_recv = recv[X_BOTH : X_BOTH + 3]
        x_from_ahead = choose(places.block == 3, row_roll(x_recv, 3), row_roll(x_ahead, -1))
        x_from_behind = choose(places.block == 0, row_roll(x_recv, -3), row_roll(x_behind, 1))
        summed = finish(
            summed,
            3,
            merge_slots(ahead_moved[3], x_from_ahead, 3, True, places),
            merge_slots(behind_moved[3], x_from_behind, 3, False, places),
        )
        messages[1].wait_recv()
        messages[2].wait_recv()
        summed = finish(
            summed,
            0,
            merge_time(t_ahead_state, recv[T_AHEAD : T_AHEAD + 3], True, places),
            merge_time(t_behind_state, recv[T_BEHIND : T_BEHIND + 3], False, places),
        )

        result = []
        for chirality in range(2):
            pair = summed[2 * chirality : 2 * chirality + 2]
            out_real = out_imag = None
            for column in range(6):
                c_real = clover[chirality, 0, :, column]
                c_imag = clover[chirality, 1, :, column]
                v_real = pair[column // 3][0][column % 3][None]
                v_imag = pair[column // 3][1][column % 3][None]
                term_real = c_real * v_real - c_imag * v_imag
                term_imag = c_real * v_imag + c_imag * v_real
                out_real = term_real if out_real is None else out_real + term_real
                out_imag = term_imag if out_imag is None else out_imag + term_imag
            result.append((out_real[:3], out_imag[:3]))
            result.append((out_real[3:], out_imag[3:]))
        return tiles_of(result)

    loads[0].wait()
    scaled[...] = fine_relax * source_ref[...]

    def prepare():
        loads[2].wait()
        clover[...] = (fine_relax * kappa_value) * clover_raw[...].astype(F32).reshape(clover.shape)
        loads[3].wait()
        for pair in range(6):
            both = vectors_raw[:, pair].astype(F32).reshape(32, 2, 8, 128)
            for side in range(2):
                place = (2 * pair + side) * 128
                matrix[:, place : place + 128] = both[:, side].reshape(256, 128).astype(BF16)
        first = lax.broadcasted_iota(jnp.int32, (256, 256), 0)
        second = lax.broadcasted_iota(jnp.int32, (256, 256), 1)
        gather[...] = jnp.where(
            (second % 128 == first // 16) & (second // 128 == (first // 8) % 2), 1.0, 0.0
        ).astype(BF16)
        scatter[...] = jnp.where(
            (first % 128 == second // 16) & (first // 128 == (second // 8) % 2), 1.0, 0.0
        ).astype(BF16)
        wide_row = lax.broadcasted_iota(jnp.int32, (16, 256), 0)
        wide_lane = lax.broadcasted_iota(jnp.int32, (16, 256), 1)
        same_row[...] = jnp.where(wide_row % 8 == wide_lane % 8, 1.0, 0.0)

    def turn():
        for c in range(12):
            part = matrix[:, 128 * c : 128 * c + 128].astype(F32)
            matrix_turned[128 * c : 128 * c + 128, :] = part.T.astype(BF16)

    def enter():
        loads[1].wait()
        for load in loads[2:]:
            load.start()
        links[...] = links_raw[...].astype(F32).reshape(links.shape)
        pl.semaphore_wait(barrier, 6)

    psi = scaled[...]
    psi = (1.0 - fine_relax) * psi + scaled[...] + clover_hopping(0, psi, enter, prepare)

    change = clover_hopping(1, psi, None, turn)
    residual = source_ref[...] - psi + (1.0 / fine_relax) * change

    stacked = jnp.stack([residual[:12], residual[12:]], axis=1).reshape(12, 16, 128).astype(BF16)
    flat = jnp.concatenate([stacked[c] for c in range(12)], axis=1)
    products = jnp.dot(flat, matrix_turned[...], preferred_element_type=F32) * same_row[...]
    high = products.astype(BF16)
    low = (products - high.astype(F32)).astype(BF16)
    sums = jnp.dot(
        jnp.concatenate([high, low], axis=0), gather[...], preferred_element_type=F32
    )
    sums = sums[:16] + sums[16:]
    coarse_real = sums[:8, :128] + sums[8:, 128:]
    coarse_imag = sums[8:, :128] - sums[:8, 128:]
    coarse_real = coarse_real + row_roll(coarse_real, 4)
    coarse_imag = coarse_imag + row_roll(coarse_imag, 4)

    own = jnp.where(places.half == 0, coarse_real, coarse_imag)
    coarse_send[...] = own
    coarse_messages = {}
    for number, target in ((1, t_prior), (2, t_next), (0, x_other), (3, y_prior), (4, y_next), (5, z_other)):
        copy = pltpu.make_async_remote_copy(
            src_ref=coarse_send,
            dst_ref=coarse_recv.at[number],
            send_sem=coarse_send_sem.at[number],
            recv_sem=coarse_recv_sem.at[number],
            device_id=target,
            device_id_type=pl.DeviceIdType.MESH,
        )
        copy.start()
        coarse_messages[number] = copy
        started.append(copy)
    settle(6)
    loads[4].wait()

    accumulated = [jnp.zeros((8, 8, 16), F32), jnp.zeros((8, 8, 16), F32)]

    def add_hop(number, tile):
        tile = coarse_relax * tile
        swapped = row_roll(tile, 4)
        e_real = jnp.where(places.half == 0, tile, swapped)[:, :16][None]
        e_imag = jnp.where(places.half == 0, swapped, tile)[:, :16][None]
        h_real, h_imag = hops_ref[number, 0], hops_ref[number, 1]
        accumulated[0] = accumulated[0] + (h_real * e_real - h_imag * e_imag)
        accumulated[1] = accumulated[1] + (h_real * e_imag + h_imag * e_real)

    coarse_messages[5].wait_recv()
    z_tile = coarse_recv[5]
    add_hop(2, z_tile)
    add_hop(3, z_tile)
    coarse_messages[3].wait_recv()
    add_hop(4, coarse_recv[3])
    coarse_messages[4].wait_recv()
    add_hop(5, coarse_recv[4])
    coarse_messages[0].wait_recv()
    x_tile = coarse_recv[0]
    add_hop(6, jnp.where(places.block == 3, row_roll(x_tile, 3), row_roll(own, -1)))
    add_hop(7, jnp.where(places.block == 0, row_roll(x_tile, -3), row_roll(own, 1)))
    coarse_messages[1].wait_recv()
    add_hop(0, coarse_recv[1])
    coarse_messages[2].wait_recv()
    add_hop(1, coarse_recv[2])

    def gathered(values):
        totals = jnp.sum(values, axis=-1, keepdims=True)
        spread = jnp.zeros((8, 128), F32)
        for pair in range(8):
            column = jnp.broadcast_to(totals[pair], (8, 128))
            spread = jnp.where(places.lane // 2 == pair, column, spread)
        return jnp.where(places.lane % 2 == places.half, spread, row_roll(spread, 4))

    first_real, first_imag = coarse_relax * coarse_real, coarse_relax * coarse_imag
    error_real = first_real + coarse_relax * (
        coarse_real - (first_real - gathered(accumulated[0]))
    )
    error_imag = first_imag + coarse_relax * (
        coarse_imag - (first_imag - gathered(accumulated[1]))
    )
    coarse_ref[0] = error_real[:4, :16]
    coarse_ref[1] = error_imag[:4, :16]

    weights = jnp.concatenate(
        [
            jnp.concatenate([error_real, error_imag], axis=0),
            jnp.concatenate([-error_imag, error_real], axis=0),
        ],
        axis=1,
    ).astype(BF16)
    spread_weights = jnp.dot(weights, scatter[...], preferred_element_type=F32)
    spread_weights = (spread_weights * same_row[...]).astype(BF16)
    correction = jnp.dot(spread_weights, matrix[...], preferred_element_type=F32)
    correction = jnp.concatenate(
        [correction[:8, 128 * c : 128 * c + 128][None] for c in range(12)]
        + [correction[8:, 128 * c : 128 * c + 128][None] for c in range(12)],
        axis=0,
    )
    psi = psi + correction

    for sweep in (2, 3):
        psi = (1.0 - fine_relax) * psi + scaled[...] + clover_hopping(sweep, psi)
    out_ref[...] = psi

    settle(0)


def deliver(out_in, coarse_in, out_ref, coarse_ref, sems):
    copies = [
        pltpu.make_async_copy(out_in, out_ref, sems.at[0]),
        pltpu.make_async_copy(coarse_in, coarse_ref, sems.at[1]),
    ]
    for copy in copies:
        copy.start()
    for copy in copies:
        copy.wait()


def rows_of_eight(values):
    count = values.size // 1024
    return values.reshape(count, 4, 2, 128).transpose(0, 2, 1, 3).reshape(count, 8, 128)


def local(source, gauge_links, clover_inverse, vectors, coarse_hops):
    source_tiles = rows_of_eight(source)
    link_tiles = rows_of_eight(gauge_links).reshape(36, 16, 128)
    clover_tiles = rows_of_eight(clover_inverse).reshape(72, 16, 128)
    vector_tiles = rows_of_eight(vectors).reshape(32, 6, 16, 128)
    hop_tiles = (
        coarse_hops.reshape(8, 2, 16, 16, 4).transpose(0, 1, 2, 4, 3).reshape(8, 2, 8, 8, 16)
    )
    out, coarse = pl.pallas_call(
        kernel,
        out_shape=(
            jax.ShapeDtypeStruct((24, 8, 128), F32),
            jax.ShapeDtypeStruct((2, 4, 16), F32),
        ),
        in_specs=[pl.BlockSpec(memory_space=pltpu.HBM)] * 5,
        out_specs=(
            pl.BlockSpec(memory_space=pltpu.VMEM),
            pl.BlockSpec(memory_space=pltpu.VMEM),
        ),
        scratch_shapes=[
            pltpu.VMEM((24, 8, 128), F32),
            pltpu.VMEM((36, 16, 128), BF16),
            pltpu.VMEM((72, 16, 128), BF16),
            pltpu.VMEM((32, 6, 16, 128), BF16),
            pltpu.VMEM((8, 2, 8, 8, 16), F32),
            pltpu.VMEM((4, 2, 3, 3, 8, 128), F32),
            pltpu.VMEM((2, 2, 6, 6, 8, 128), F32),
            pltpu.VMEM((256, 1536), BF16),
            pltpu.VMEM((1536, 256), BF16),
            pltpu.VMEM((256, 256), BF16),
            pltpu.VMEM((256, 256), BF16),
            pltpu.VMEM((16, 256), F32),
            pltpu.VMEM((24, 8, 128), F32),
            pltpu.VMEM((4, TILES, 8, 128), F32),
            pltpu.VMEM((4, TILES, 8, 128), F32),
            pltpu.VMEM((8, 128), F32),
            pltpu.VMEM((6, 8, 128), F32),
            pltpu.SemaphoreType.DMA((5,)),
            pltpu.SemaphoreType.DMA((4, 6)),
            pltpu.SemaphoreType.DMA((4, 6)),
            pltpu.SemaphoreType.DMA((6,)),
            pltpu.SemaphoreType.DMA((6,)),
        ],
        compiler_params=pltpu.CompilerParams(
            collective_id=0, has_side_effects=True, vmem_limit_bytes=55040 * 1024
        ),
    )(source_tiles, link_tiles, clover_tiles, vector_tiles, hop_tiles)
    out, coarse = pl.pallas_call(
        deliver,
        out_shape=(
            jax.ShapeDtypeStruct((24, 8, 128), F32),
            jax.ShapeDtypeStruct((2, 4, 16), F32),
        ),
        in_specs=[pl.BlockSpec(memory_space=pl.ANY)] * 2,
        out_specs=[pl.BlockSpec(memory_space=pl.ANY)] * 2,
        scratch_shapes=[pltpu.SemaphoreType.DMA((2,))],
        compiler_params=pltpu.CompilerParams(vmem_limit_bytes=1024 * 1024),
    )(out, coarse)
    solution_out = (
        out.reshape(24, 2, 4, 128).transpose(0, 2, 1, 3).reshape(2, 4, 3, 1, 1, 1, 4, 256)
    )
    coarse_out = coarse.transpose(0, 2, 1).reshape(2, 16, 1, 1, 1, 4)
    return solution_out, coarse_out


def solution(mesh):
    return jax.shard_map(
        local,
        mesh=mesh,
        in_specs=(
            P(None, None, None, "ta", "gz", "gy", "gx", None),
            P(None, None, None, None, "ta", "gz", "gy", "gx", None),
            P(None, None, None, None, "ta", "gz", "gy", "gx", None),
            P(None, None, None, None, "ta", "gz", "gy", "gx", None),
            P(None, None, None, None, "ta", "gz", "gy", "gx"),
        ),
        out_specs=(
            P(None, None, None, "ta", "gz", "gy", "gx", None),
            P(None, None, "ta", "gz", "gy", "gx"),
        ),
        check_vma=False,
    )
```

```python
import jax
import jax.numpy as jnp
from jax import lax
from jax.experimental import pallas as pl
from jax.experimental.pallas import tpu as pltpu
from jax.sharding import PartitionSpec as P


kappa_value = 0.125
fine_relax = 0.8
coarse_relax = 0.7

F32 = jnp.float32
BF16 = jnp.bfloat16

B_ROWS = (((0, 0), (1, 0)), ((0, 3), (1, 1)), ((1, 2), (0, 0)), ((1, 3), (0, 3)))
B_ADJOINT_ROWS = (((0, 0), (1, 0)), ((0, 1), (1, 3)), ((1, 0), (0, 2)), ((1, 1), (0, 1)))

T_AHEAD, T_BEHIND, Y_AHEAD, Y_BEHIND, Z_BOTH, X_BOTH = 0, 3, 6, 9, 12, 18
TILES = 21


def plus_unit(target, unit, value):
    if unit == 0:
        return target[0] + value[0], target[1] + value[1]
    if unit == 1:
        return target[0] - value[1], target[1] + value[0]
    if unit == 2:
        return target[0] - value[0], target[1] - value[1]
    return target[0] + value[1], target[1] - value[0]


def project(spins, direction, sign):
    halves = []
    for row in range(2):
        column, unit = B_ROWS[direction][row]
        unit = unit if sign > 0 else (unit + 2) % 4
        halves.append(plus_unit(spins[row], unit, spins[2 + column]))
    return jnp.concatenate([halves[0][0], halves[1][0], halves[0][1], halves[1][1]], axis=0)


def lift(summed, half, direction, sign):
    pair = [(half[0:3], half[6:9]), (half[3:6], half[9:12])]
    result = []
    for row in range(2):
        result.append(plus_unit(summed[row], 0, pair[row]))
    for row in range(2):
        column, unit = B_ADJOINT_ROWS[direction][row]
        unit = unit if sign > 0 else (unit + 2) % 4
        result.append(plus_unit(summed[2 + row], unit, pair[column]))
    return result


def link_times(links, direction, half, dagger):
    real_part = half[:6].reshape(2, 3, 8, 128)
    imag_part = half[6:].reshape(2, 3, 8, 128)
    out_real = out_imag = None
    for b in range(3):
        if dagger:
            u_real, u_imag = links[direction, 0, b], links[direction, 1, b]
        else:
            u_real, u_imag = links[direction, 0, :, b], links[direction, 1, :, b]
        u_real, u_imag = u_real[None], u_imag[None]
        v_real, v_imag = real_part[:, b][:, None], imag_part[:, b][:, None]
        if dagger:
            term_real = u_real * v_real + u_imag * v_imag
            term_imag = u_real * v_imag - u_imag * v_real
        else:
            term_real = u_real * v_real - u_imag * v_imag
            term_imag = u_real * v_imag + u_imag * v_real
        out_real = term_real if out_real is None else out_real + term_real
        out_imag = term_imag if out_imag is None else out_imag + term_imag
    return jnp.concatenate([out_real.reshape(6, 8, 128), out_imag.reshape(6, 8, 128)], axis=0)


def lane_roll(values, shift):
    shift = shift % 128
    return values if shift == 0 else pltpu.roll(values, shift, values.ndim - 1)


def row_roll(values, shift):
    shift = shift % 8
    return values if shift == 0 else pltpu.roll(values, shift, values.ndim - 2)


class Places:
    def __init__(self):
        row = lax.broadcasted_iota(jnp.int32, (8, 128), 0)
        lane = lax.broadcasted_iota(jnp.int32, (8, 128), 1)
        self.row, self.lane = row, lane
        self.block = row % 4
        self.half = row // 4
        self.parity = lane // 64
        self.slot = {1: (lane // 16) % 4, 2: (lane // 4) % 4, 3: lane % 4}


STRIDE = {1: 16, 2: 4, 3: 1}


def choose(mask, first, second):
    return jnp.where(jnp.broadcast_to(mask[None], first.shape), first, second)


def pack_slots(half, direction, ahead, places):
    stride, slot = STRIDE[direction], places.slot[direction]
    fours = half.reshape(3, 4, 8, 128)
    packed = fours[:, 0]
    for k in range(1, 4):
        if ahead:
            packed = choose(slot == k, lane_roll(fours[:, k], stride * k), packed)
        else:
            packed = choose(slot == 3 - k, lane_roll(fours[:, k], -stride * k), packed)
    return packed


def merge_slots(rolled, packed, direction, ahead, places):
    stride, slot = STRIDE[direction], places.slot[direction]
    fours = rolled.reshape(3, 4, 8, 128)
    merged = []
    for k in range(4):
        if ahead:
            merged.append(choose(slot == 3, lane_roll(packed, stride * (3 - k)), fours[:, k]))
        else:
            merged.append(choose(slot == 0, lane_roll(packed, -stride * (3 - k)), fours[:, k]))
    return jnp.stack(merged, axis=1).reshape(12, 8, 128)


def pack_time(half, ahead, places):
    edge = places.parity == (0 if ahead else 1)
    edge_rows = places.half == (0 if ahead else 1)
    pairs = half.reshape(6, 2, 8, 128)
    first, second = pairs[:, 0], lane_roll(pairs[:, 1], 64)
    paired = choose(edge, first, second).reshape(3, 2, 8, 128)
    paired_first, paired_second = paired[:, 0], row_roll(paired[:, 1], 4)
    packed = choose(edge_rows, paired_first, paired_second)
    return packed, (first, second, paired_first, paired_second)


def merge_time(state, packed, ahead, places):
    edge = places.parity == (0 if ahead else 1)
    edge_rows = places.half == (0 if ahead else 1)
    first, second, paired_first, paired_second = state
    next_first = row_roll(choose(edge_rows, packed, paired_first), 4)
    next_second = choose(edge_rows, paired_second, packed)
    moved = jnp.stack([next_first, next_second], axis=1).reshape(6, 8, 128)
    out_first = lane_roll(choose(edge, moved, first), 64)
    out_second = choose(edge, second, moved)
    return jnp.stack([out_first, out_second], axis=1).reshape(12, 8, 128)


def spins_of(values):
    return [(values[3 * s : 3 * s + 3], values[12 + 3 * s : 15 + 3 * s]) for s in range(4)]


def tiles_of(spins):
    return jnp.concatenate([spin[0] for spin in spins] + [spin[1] for spin in spins], axis=0)


def kernel(
    source_hbm,
    links_hbm,
    clover_hbm,
    vectors_hbm,
    hops_hbm,
    out_ref,
    coarse_ref,
    source_ref,
    links_raw,
    clover_raw,
    vectors_raw,
    hops_ref,
    links,
    clover,
    wide,
    scaled,
    send_buffer,
    recv_buffer,
    coarse_send,
    coarse_recv,
    load_sem,
    send_sem,
    recv_sem,
    coarse_send_sem,
    coarse_recv_sem,
):
    loads = []
    for index, (origin, target) in enumerate(
        (
            (source_hbm, source_ref),
            (links_hbm, links_raw),
            (clover_hbm, clover_raw),
            (vectors_hbm, vectors_raw),
            (hops_hbm, hops_ref),
        )
    ):
        loads.append(pltpu.make_async_copy(origin, target, load_sem.at[index]))

    def around(axis, step):
        count = lax.axis_size(axis)
        return {axis: lax.rem(lax.axis_index(axis) + (step + count), count)}

    t_next, t_prior = around("ta", 1), around("ta", -1)
    y_next, y_prior = around("gy", 1), around("gy", -1)
    z_other, x_other = around("gz", 1), around("gx", 1)

    barrier = pltpu.get_barrier_semaphore()
    for neighbour in (x_other, t_next, t_prior, y_next, y_prior, z_other):
        pl.semaphore_signal(
            barrier, inc=1, device_id=neighbour, device_id_type=pl.DeviceIdType.MESH
        )

    loads[0].start()
    loads[1].start()
    places = Places()

    def message(sweep, number, start, count, target):
        window = pl.ds(start, count)
        return pltpu.make_async_remote_copy(
            src_ref=send_buffer.at[sweep, window],
            dst_ref=recv_buffer.at[sweep, window],
            send_sem=send_sem.at[sweep, number],
            recv_sem=recv_sem.at[sweep, number],
            device_id=target,
            device_id_type=pl.DeviceIdType.MESH,
        )

    started = []

    def settle(keep):
        while len(started) > keep:
            started.pop(0).wait_send()

    def clover_hopping(sweep, psi, before_send=None, while_waiting=None):
        spins = spins_of(psi)
        send = send_buffer.at[sweep]
        recv = recv_buffer.at[sweep]
        ahead, behind, messages = {}, {}, {}

        def halves(mu):
            ahead[mu] = project(spins, mu, -1)
            behind[mu] = link_times(links, mu, project(spins, mu, 1), True)

        def dispatch(number, start, count, target):
            messages[number] = message(sweep, number, start, count, target)
            messages[number].start()
            started.append(messages[number])

        halves(3)
        x_ahead = pack_slots(ahead[3], 3, True, places)
        x_behind = pack_slots(behind[3], 3, False, places)
        send[X_BOTH : X_BOTH + 3] = choose(places.block == 0, x_ahead, x_behind)
        if before_send is not None:
            before_send()
        dispatch(0, X_BOTH, 3, x_other)
        ahead[0] = project(spins, 0, -1)
        t_ahead, t_ahead_state = pack_time(ahead[0], True, places)
        send[T_AHEAD : T_AHEAD + 3] = t_ahead
        dispatch(1, T_AHEAD, 3, t_prior)
        behind[0] = link_times(links, 0, project(spins, 0, 1), True)
        t_behind, t_behind_state = pack_time(behind[0], False, places)
        send[T_BEHIND : T_BEHIND + 3] = t_behind
        dispatch(2, T_BEHIND, 3, t_next)
        halves(2)
        send[Y_AHEAD : Y_AHEAD + 3] = pack_slots(ahead[2], 2, True, places)
        dispatch(3, Y_AHEAD, 3, y_prior)
        send[Y_BEHIND : Y_BEHIND + 3] = pack_slots(behind[2], 2, False, places)
        dispatch(4, Y_BEHIND, 3, y_next)
        halves(1)
        send[Z_BOTH : Z_BOTH + 3] = pack_slots(ahead[1], 1, True, places)
        send[Z_BOTH + 3 : Z_BOTH + 6] = pack_slots(behind[1], 1, False, places)
        dispatch(5, Z_BOTH, 6, z_other)
        settle(6)
        if while_waiting is not None:
            while_waiting()

        ahead_moved = {mu: lane_roll(ahead[mu], -STRIDE[mu]) for mu in (1, 2, 3)}
        behind_moved = {mu: lane_roll(behind[mu], STRIDE[mu]) for mu in (1, 2, 3)}
        zero = jnp.zeros((3, 8, 128), F32)
        summed = [(zero, zero)] * 4

        def finish(summed, mu, from_ahead, from_behind):
            summed = lift(summed, link_times(links, mu, from_ahead, False), mu, -1)
            return lift(summed, from_behind, mu, 1)

        messages[5].wait_recv()
        summed = finish(
            summed,
            1,
            merge_slots(ahead_moved[1], recv[Z_BOTH : Z_BOTH + 3], 1, True, places),
            merge_slots(behind_moved[1], recv[Z_BOTH + 3 : Z_BOTH + 6], 1, False, places),
        )
        messages[3].wait_recv()
        messages[4].wait_recv()
        summed = finish(
            summed,
            2,
            merge_slots(ahead_moved[2], recv[Y_AHEAD : Y_AHEAD + 3], 2, True, places),
            merge_slots(behind_moved[2], recv[Y_BEHIND : Y_BEHIND + 3], 2, False, places),
        )
        messages[0].wait_recv()
        x_recv = recv[X_BOTH : X_BOTH + 3]
        x_from_ahead = choose(places.block == 3, row_roll(x_recv, 3), row_roll(x_ahead, -1))
        x_from_behind = choose(places.block == 0, row_roll(x_recv, -3), row_roll(x_behind, 1))
        summed = finish(
            summed,
            3,
            merge_slots(ahead_moved[3], x_from_ahead, 3, True, places),
            merge_slots(behind_moved[3], x_from_behind, 3, False, places),
        )
        messages[1].wait_recv()
        messages[2].wait_recv()
        summed = finish(
            summed,
            0,
            merge_time(t_ahead_state, recv[T_AHEAD : T_AHEAD + 3], True, places),
            merge_time(t_behind_state, recv[T_BEHIND : T_BEHIND + 3], False, places),
        )

        result = []
        for chirality in range(2):
            pair = summed[2 * chirality : 2 * chirality + 2]
            out_real = out_imag = None
            for column in range(6):
                c_real = clover[chirality, 0, :, column]
                c_imag = clover[chirality, 1, :, column]
                v_real = pair[column // 3][0][column % 3][None]
                v_imag = pair[column // 3][1][column % 3][None]
                term_real = c_real * v_real - c_imag * v_imag
                term_imag = c_real * v_imag + c_imag * v_real
                out_real = term_real if out_real is None else out_real + term_real
                out_imag = term_imag if out_imag is None else out_imag + term_imag
            result.append((out_real[:3], out_imag[:3]))
            result.append((out_real[3:], out_imag[3:]))
        return tiles_of(result)

    loads[0].wait()
    scaled[...] = fine_relax * source_ref[...]

    def prepare():
        for load in loads[2:]:
            load.start()
        loads[2].wait()
        clover[...] = (fine_relax * kappa_value) * clover_raw[...].astype(F32).reshape(clover.shape)
        loads[3].wait()
        wide[...] = vectors_raw[...].astype(F32).reshape(wide.shape)

    def enter():
        pl.semaphore_wait(barrier, 6)

    loads[1].wait()
    links[...] = links_raw[...].astype(F32).reshape(links.shape)

    psi = scaled[...]
    psi = (1.0 - fine_relax) * psi + scaled[...] + clover_hopping(0, psi, enter, prepare)

    change = clover_hopping(1, psi)
    residual = source_ref[...] - psi + (1.0 / fine_relax) * change

    rounded = residual.astype(BF16).astype(F32)
    rest_real, rest_imag = rounded[:12], rounded[12:]
    reals, imags = [], []
    for k in range(16):
        v_real, v_imag = wide[k, 0], wide[k, 1]
        reals.append(jnp.sum(v_real * rest_real + v_imag * rest_imag, axis=0))
        imags.append(jnp.sum(v_real * rest_imag - v_imag * rest_real, axis=0))

    def over_lanes(tile):
        total = jnp.broadcast_to(jnp.sum(tile, axis=-1, keepdims=True), (8, 128))
        return total + row_roll(total, 4)

    def into_lanes(columns):
        layer = list(columns)
        bit = 1
        while len(layer) > 1:
            odd = (places.lane // bit) % 2 == 1
            layer = [
                jnp.where(odd, layer[n + 1], layer[n]) for n in range(0, len(layer), 2)
            ]
            bit *= 2
        return layer[0]

    reals = [over_lanes(tile) for tile in reals]
    imags = [over_lanes(tile) for tile in imags]
    coarse_real, coarse_imag = into_lanes(reals), into_lanes(imags)

    own = jnp.where(places.half == 0, coarse_real, coarse_imag)
    coarse_send[...] = own
    coarse_messages = {}
    for number, target in ((1, t_prior), (2, t_next), (0, x_other), (3, y_prior), (4, y_next), (5, z_other)):
        copy = pltpu.make_async_remote_copy(
            src_ref=coarse_send,
            dst_ref=coarse_recv.at[number],
            send_sem=coarse_send_sem.at[number],
            recv_sem=coarse_recv_sem.at[number],
            device_id=target,
            device_id_type=pl.DeviceIdType.MESH,
        )
        copy.start()
        coarse_messages[number] = copy
        started.append(copy)
    settle(6)
    loads[4].wait()

    accumulated = [jnp.zeros((8, 8, 16), F32), jnp.zeros((8, 8, 16), F32)]

    def add_hop(number, tile):
        tile = coarse_relax * tile
        swapped = row_roll(tile, 4)
        e_real = jnp.where(places.half == 0, tile, swapped)[:, :16][None]
        e_imag = jnp.where(places.half == 0, swapped, tile)[:, :16][None]
        h_real, h_imag = hops_ref[number, 0], hops_ref[number, 1]
        accumulated[0] = accumulated[0] + (h_real * e_real - h_imag * e_imag)
        accumulated[1] = accumulated[1] + (h_real * e_imag + h_imag * e_real)

    coarse_messages[5].wait_recv()
    z_tile = coarse_recv[5]
    add_hop(2, z_tile)
    add_hop(3, z_tile)
    coarse_messages[3].wait_recv()
    add_hop(4, coarse_recv[3])
    coarse_messages[4].wait_recv()
    add_hop(5, coarse_recv[4])
    coarse_messages[0].wait_recv()
    x_tile = coarse_recv[0]
    add_hop(6, jnp.where(places.block == 3, row_roll(x_tile, 3), row_roll(own, -1)))
    add_hop(7, jnp.where(places.block == 0, row_roll(x_tile, -3), row_roll(own, 1)))
    coarse_messages[1].wait_recv()
    add_hop(0, coarse_recv[1])
    coarse_messages[2].wait_recv()
    add_hop(1, coarse_recv[2])

    def errors(sources, values):
        spread = []
        for pair in range(8):
            total = jnp.broadcast_to(
                jnp.sum(values[pair], axis=-1, keepdims=True), (8, 128)
            )
            swapped = row_roll(total, 4)
            spread.append(jnp.where(places.half == 0, total, swapped))
            spread.append(jnp.where(places.half == 0, swapped, total))
        result = []
        for k in range(16):
            first = coarse_relax * sources[k]
            result.append(first + coarse_relax * ((sources[k] - first) + spread[k]))
        return result

    error_real = errors(reals, accumulated[0])
    error_imag = errors(imags, accumulated[1])

    add_real, add_imag = psi[:12], psi[12:]
    for k in range(16):
        v_real, v_imag = wide[k, 0], wide[k, 1]
        e_real = error_real[k].astype(BF16).astype(F32)[None]
        e_imag = error_imag[k].astype(BF16).astype(F32)[None]
        add_real = add_real + (v_real * e_real - v_imag * e_imag)
        add_imag = add_imag + (v_real * e_imag + v_imag * e_real)
    psi = jnp.concatenate([add_real, add_imag], axis=0)

    def hand_out():
        coarse_ref[0] = into_lanes(error_real)[:4, :16]
        coarse_ref[1] = into_lanes(error_imag)[:4, :16]

    for sweep in (2, 3):
        psi = (
            (1.0 - fine_relax) * psi
            + scaled[...]
            + clover_hopping(sweep, psi, None, hand_out if sweep == 2 else None)
        )
    out_ref[...] = psi

    settle(0)


def deliver(out_in, coarse_in, out_ref, coarse_ref, sems):
    copies = [
        pltpu.make_async_copy(out_in, out_ref, sems.at[0]),
        pltpu.make_async_copy(coarse_in, coarse_ref, sems.at[1]),
    ]
    for copy in copies:
        copy.start()
    for copy in copies:
        copy.wait()


def rows_of_eight(values):
    count = values.size // 1024
    return values.reshape(count, 4, 2, 128).transpose(0, 2, 1, 3).reshape(count, 8, 128)


def local(source, gauge_links, clover_inverse, vectors, coarse_hops):
    source_tiles = rows_of_eight(source)
    link_tiles = rows_of_eight(gauge_links).reshape(36, 16, 128)
    clover_tiles = rows_of_eight(clover_inverse).reshape(72, 16, 128)
    vector_tiles = rows_of_eight(vectors).reshape(32, 6, 16, 128)
    hop_tiles = (
        coarse_hops.reshape(8, 2, 16, 16, 4).transpose(0, 1, 2, 4, 3).reshape(8, 2, 8, 8, 16)
    )
    out, coarse = pl.pallas_call(
        kernel,
        out_shape=(
            jax.ShapeDtypeStruct((24, 8, 128), F32),
            jax.ShapeDtypeStruct((2, 4, 16), F32),
        ),
        in_specs=[pl.BlockSpec(memory_space=pltpu.HBM)] * 5,
        out_specs=(
            pl.BlockSpec(memory_space=pltpu.VMEM),
            pl.BlockSpec(memory_space=pltpu.VMEM),
        ),
        scratch_shapes=[
            pltpu.VMEM((24, 8, 128), F32),
            pltpu.VMEM((36, 16, 128), BF16),
            pltpu.VMEM((72, 16, 128), BF16),
            pltpu.VMEM((32, 6, 16, 128), BF16),
            pltpu.VMEM((8, 2, 8, 8, 16), F32),
            pltpu.VMEM((4, 2, 3, 3, 8, 128), F32),
            pltpu.VMEM((2, 2, 6, 6, 8, 128), F32),
            pltpu.VMEM((16, 2, 12, 8, 128), F32),
            pltpu.VMEM((24, 8, 128), F32),
            pltpu.VMEM((4, TILES, 8, 128), F32),
            pltpu.VMEM((4, TILES, 8, 128), F32),
            pltpu.VMEM((8, 128), F32),
            pltpu.VMEM((6, 8, 128), F32),
            pltpu.SemaphoreType.DMA((5,)),
            pltpu.SemaphoreType.DMA((4, 6)),
            pltpu.SemaphoreType.DMA((4, 6)),
            pltpu.SemaphoreType.DMA((6,)),
            pltpu.SemaphoreType.DMA((6,)),
        ],
        compiler_params=pltpu.CompilerParams(
            collective_id=0, has_side_effects=True, vmem_limit_bytes=55040 * 1024
        ),
    )(source_tiles, link_tiles, clover_tiles, vector_tiles, hop_tiles)
    out, coarse = pl.pallas_call(
        deliver,
        out_shape=(
            jax.ShapeDtypeStruct((24, 8, 128), F32),
            jax.ShapeDtypeStruct((2, 4, 16), F32),
        ),
        in_specs=[pl.BlockSpec(memory_space=pl.ANY)] * 2,
        out_specs=[pl.BlockSpec(memory_space=pl.ANY)] * 2,
        scratch_shapes=[pltpu.SemaphoreType.DMA((2,))],
        compiler_params=pltpu.CompilerParams(vmem_limit_bytes=1024 * 1024),
    )(out, coarse)
    solution_out = (
        out.reshape(24, 2, 4, 128).transpose(0, 2, 1, 3).reshape(2, 4, 3, 1, 1, 1, 4, 256)
    )
    coarse_out = coarse.transpose(0, 2, 1).reshape(2, 16, 1, 1, 1, 4)
    return solution_out, coarse_out


def solution(mesh):
    return jax.shard_map(
        local,
        mesh=mesh,
        in_specs=(
            P(None, None, None, "ta", "gz", "gy", "gx", None),
            P(None, None, None, None, "ta", "gz", "gy", "gx", None),
            P(None, None, None, None, "ta", "gz", "gy", "gx", None),
            P(None, None, None, None, "ta", "gz", "gy", "gx", None),
            P(None, None, None, None, "ta", "gz", "gy", "gx"),
        ),
        out_specs=(
            P(None, None, None, "ta", "gz", "gy", "gx", None),
            P(None, None, "ta", "gz", "gy", "gx"),
        ),
        check_vma=False,
    )
```

```python
import jax
import jax.numpy as jnp
from jax import lax
from jax.experimental import pallas as pl
from jax.experimental.pallas import tpu as pltpu
from jax.sharding import PartitionSpec as P


kappa_value = 0.125
fine_relax = 0.8
coarse_relax = 0.7

F32 = jnp.float32
BF16 = jnp.bfloat16

B_ROWS = (((0, 0), (1, 0)), ((0, 3), (1, 1)), ((1, 2), (0, 0)), ((1, 3), (0, 3)))
B_ADJOINT_ROWS = (((0, 0), (1, 0)), ((0, 1), (1, 3)), ((1, 0), (0, 2)), ((1, 1), (0, 1)))

T_AHEAD, T_BEHIND, Y_AHEAD, Y_BEHIND, Z_BOTH, X_BOTH = 0, 3, 6, 9, 12, 18
TILES = 21


def plus_unit(target, unit, value):
    if unit == 0:
        return target[0] + value[0], target[1] + value[1]
    if unit == 1:
        return target[0] - value[1], target[1] + value[0]
    if unit == 2:
        return target[0] - value[0], target[1] - value[1]
    return target[0] + value[1], target[1] - value[0]


def project(spins, direction, sign):
    halves = []
    for row in range(2):
        column, unit = B_ROWS[direction][row]
        unit = unit if sign > 0 else (unit + 2) % 4
        halves.append(plus_unit(spins[row], unit, spins[2 + column]))
    return jnp.concatenate([halves[0][0], halves[1][0], halves[0][1], halves[1][1]], axis=0)


def lift(summed, half, direction, sign):
    pair = [(half[0:3], half[6:9]), (half[3:6], half[9:12])]
    result = []
    for row in range(2):
        result.append(plus_unit(summed[row], 0, pair[row]))
    for row in range(2):
        column, unit = B_ADJOINT_ROWS[direction][row]
        unit = unit if sign > 0 else (unit + 2) % 4
        result.append(plus_unit(summed[2 + row], unit, pair[column]))
    return result


def link_times(links, direction, half, dagger):
    real_part = half[:6].reshape(2, 3, 8, 128)
    imag_part = half[6:].reshape(2, 3, 8, 128)
    out_real = out_imag = None
    for b in range(3):
        if dagger:
            u_real, u_imag = links[direction, 0, b], links[direction, 1, b]
        else:
            u_real, u_imag = links[direction, 0, :, b], links[direction, 1, :, b]
        u_real, u_imag = u_real[None], u_imag[None]
        v_real, v_imag = real_part[:, b][:, None], imag_part[:, b][:, None]
        if dagger:
            term_real = u_real * v_real + u_imag * v_imag
            term_imag = u_real * v_imag - u_imag * v_real
        else:
            term_real = u_real * v_real - u_imag * v_imag
            term_imag = u_real * v_imag + u_imag * v_real
        out_real = term_real if out_real is None else out_real + term_real
        out_imag = term_imag if out_imag is None else out_imag + term_imag
    return jnp.concatenate([out_real.reshape(6, 8, 128), out_imag.reshape(6, 8, 128)], axis=0)


def lane_roll(values, shift):
    shift = shift % 128
    return values if shift == 0 else pltpu.roll(values, shift, values.ndim - 1)


def row_roll(values, shift):
    shift = shift % 8
    return values if shift == 0 else pltpu.roll(values, shift, values.ndim - 2)


class Places:
    def __init__(self):
        row = lax.broadcasted_iota(jnp.int32, (8, 128), 0)
        lane = lax.broadcasted_iota(jnp.int32, (8, 128), 1)
        self.row, self.lane = row, lane
        self.block = row % 4
        self.half = row // 4
        self.parity = lane // 64
        self.slot = {1: (lane // 16) % 4, 2: (lane // 4) % 4, 3: lane % 4}


STRIDE = {1: 16, 2: 4, 3: 1}


def choose(mask, first, second):
    return jnp.where(jnp.broadcast_to(mask[None], first.shape), first, second)


def pack_slots(half, direction, ahead, places):
    stride, slot = STRIDE[direction], places.slot[direction]
    fours = half.reshape(3, 4, 8, 128)
    packed = fours[:, 0]
    for k in range(1, 4):
        if ahead:
            packed = choose(slot == k, lane_roll(fours[:, k], stride * k), packed)
        else:
            packed = choose(slot == 3 - k, lane_roll(fours[:, k], -stride * k), packed)
    return packed


def merge_slots(rolled, packed, direction, ahead, places):
    stride, slot = STRIDE[direction], places.slot[direction]
    fours = rolled.reshape(3, 4, 8, 128)
    merged = []
    for k in range(4):
        if ahead:
            merged.append(choose(slot == 3, lane_roll(packed, stride * (3 - k)), fours[:, k]))
        else:
            merged.append(choose(slot == 0, lane_roll(packed, -stride * (3 - k)), fours[:, k]))
    return jnp.stack(merged, axis=1).reshape(12, 8, 128)


def pack_time(half, ahead, places):
    edge = places.parity == (0 if ahead else 1)
    edge_rows = places.half == (0 if ahead else 1)
    pairs = half.reshape(6, 2, 8, 128)
    first, second = pairs[:, 0], lane_roll(pairs[:, 1], 64)
    paired = choose(edge, first, second).reshape(3, 2, 8, 128)
    paired_first, paired_second = paired[:, 0], row_roll(paired[:, 1], 4)
    packed = choose(edge_rows, paired_first, paired_second)
    return packed, (first, second, paired_first, paired_second)


def merge_time(state, packed, ahead, places):
    edge = places.parity == (0 if ahead else 1)
    edge_rows = places.half == (0 if ahead else 1)
    first, second, paired_first, paired_second = state
    next_first = row_roll(choose(edge_rows, packed, paired_first), 4)
    next_second = choose(edge_rows, paired_second, packed)
    moved = jnp.stack([next_first, next_second], axis=1).reshape(6, 8, 128)
    out_first = lane_roll(choose(edge, moved, first), 64)
    out_second = choose(edge, second, moved)
    return jnp.stack([out_first, out_second], axis=1).reshape(12, 8, 128)


def spins_of(values):
    return [(values[3 * s : 3 * s + 3], values[12 + 3 * s : 15 + 3 * s]) for s in range(4)]


def tiles_of(spins):
    return jnp.concatenate([spin[0] for spin in spins] + [spin[1] for spin in spins], axis=0)


def kernel(
    source_hbm,
    links_hbm,
    clover_hbm,
    vectors_hbm,
    hops_hbm,
    out_ref,
    coarse_ref,
    source_ref,
    links_raw,
    clover_raw,
    vectors_raw,
    hops_ref,
    links,
    clover,
    wide,
    faces,
    scaled,
    send_buffer,
    recv_buffer,
    coarse_send,
    coarse_recv,
    load_sem,
    send_sem,
    recv_sem,
    coarse_send_sem,
    coarse_recv_sem,
):
    loads = []
    for index, (origin, target) in enumerate(
        (
            (source_hbm, source_ref),
            (links_hbm, links_raw),
            (clover_hbm, clover_raw),
            (vectors_hbm, vectors_raw),
            (hops_hbm, hops_ref),
        )
    ):
        loads.append(pltpu.make_async_copy(origin, target, load_sem.at[index]))

    def around(axis, step):
        count = lax.axis_size(axis)
        return {axis: lax.rem(lax.axis_index(axis) + (step + count), count)}

    t_next, t_prior = around("ta", 1), around("ta", -1)
    y_next, y_prior = around("gy", 1), around("gy", -1)
    z_other, x_other = around("gz", 1), around("gx", 1)

    barrier = pltpu.get_barrier_semaphore()
    for neighbour in (x_other, t_next, t_prior, y_next, y_prior, z_other):
        pl.semaphore_signal(
            barrier, inc=1, device_id=neighbour, device_id_type=pl.DeviceIdType.MESH
        )

    loads[0].start()
    loads[1].start()
    places = Places()

    def message(sweep, number, start, count, target):
        window = pl.ds(start, count)
        return pltpu.make_async_remote_copy(
            src_ref=send_buffer.at[sweep, window],
            dst_ref=recv_buffer.at[sweep, window],
            send_sem=send_sem.at[sweep, number],
            recv_sem=recv_sem.at[sweep, number],
            device_id=target,
            device_id_type=pl.DeviceIdType.MESH,
        )

    started = []

    def settle(keep):
        while len(started) > keep:
            started.pop(0).wait_send()

    def clover_hopping(sweep, psi, before_send=None, while_waiting=None, sent=()):
        spins = spins_of(psi)
        send = send_buffer.at[sweep]
        recv = recv_buffer.at[sweep]
        ahead, behind, messages = {}, {}, {}

        def halves(mu):
            ahead[mu] = project(spins, mu, -1)
            behind[mu] = link_times(links, mu, project(spins, mu, 1), True)

        def dispatch(number, start, count, target):
            if number in sent:
                messages[number] = sent[number]
                return
            messages[number] = message(sweep, number, start, count, target)
            started.append(messages[number])
            if before_send is None:
                messages[number].start()

        halves(3)
        x_ahead = pack_slots(ahead[3], 3, True, places)
        x_behind = pack_slots(behind[3], 3, False, places)
        if 0 not in sent:
            send[X_BOTH : X_BOTH + 3] = choose(places.block == 0, x_ahead, x_behind)
        dispatch(0, X_BOTH, 3, x_other)
        ahead[0] = project(spins, 0, -1)
        t_ahead, t_ahead_state = pack_time(ahead[0], True, places)
        if 1 not in sent:
            send[T_AHEAD : T_AHEAD + 3] = t_ahead
        dispatch(1, T_AHEAD, 3, t_prior)
        behind[0] = link_times(links, 0, project(spins, 0, 1), True)
        t_behind, t_behind_state = pack_time(behind[0], False, places)
        if 2 not in sent:
            send[T_BEHIND : T_BEHIND + 3] = t_behind
        dispatch(2, T_BEHIND, 3, t_next)
        halves(2)
        send[Y_AHEAD : Y_AHEAD + 3] = pack_slots(ahead[2], 2, True, places)
        dispatch(3, Y_AHEAD, 3, y_prior)
        send[Y_BEHIND : Y_BEHIND + 3] = pack_slots(behind[2], 2, False, places)
        dispatch(4, Y_BEHIND, 3, y_next)
        halves(1)
        send[Z_BOTH : Z_BOTH + 3] = pack_slots(ahead[1], 1, True, places)
        send[Z_BOTH + 3 : Z_BOTH + 6] = pack_slots(behind[1], 1, False, places)
        dispatch(5, Z_BOTH, 6, z_other)
        if before_send is not None:
            before_send()
            for copy in messages.values():
                copy.start()
        settle(6)
        if while_waiting is not None:
            while_waiting()

        ahead_moved = {mu: lane_roll(ahead[mu], -STRIDE[mu]) for mu in (1, 2, 3)}
        behind_moved = {mu: lane_roll(behind[mu], STRIDE[mu]) for mu in (1, 2, 3)}
        zero = jnp.zeros((3, 8, 128), F32)
        summed = [(zero, zero)] * 4

        def finish(summed, mu, from_ahead, from_behind):
            summed = lift(summed, link_times(links, mu, from_ahead, False), mu, -1)
            return lift(summed, from_behind, mu, 1)

        messages[5].wait_recv()
        summed = finish(
            summed,
            1,
            merge_slots(ahead_moved[1], recv[Z_BOTH : Z_BOTH + 3], 1, True, places),
            merge_slots(behind_moved[1], recv[Z_BOTH + 3 : Z_BOTH + 6], 1, False, places),
        )
        messages[3].wait_recv()
        messages[4].wait_recv()
        summed = finish(
            summed,
            2,
            merge_slots(ahead_moved[2], recv[Y_AHEAD : Y_AHEAD + 3], 2, True, places),
            merge_slots(behind_moved[2], recv[Y_BEHIND : Y_BEHIND + 3], 2, False, places),
        )
        messages[0].wait_recv()
        x_recv = recv[X_BOTH : X_BOTH + 3]
        x_from_ahead = choose(places.block == 3, row_roll(x_recv, 3), row_roll(x_ahead, -1))
        x_from_behind = choose(places.block == 0, row_roll(x_recv, -3), row_roll(x_behind, 1))
        summed = finish(
            summed,
            3,
            merge_slots(ahead_moved[3], x_from_ahead, 3, True, places),
            merge_slots(behind_moved[3], x_from_behind, 3, False, places),
        )
        messages[1].wait_recv()
        messages[2].wait_recv()
        summed = finish(
            summed,
            0,
            merge_time(t_ahead_state, recv[T_AHEAD : T_AHEAD + 3], True, places),
            merge_time(t_behind_state, recv[T_BEHIND : T_BEHIND + 3], False, places),
        )

        result = []
        for chirality in range(2):
            pair = summed[2 * chirality : 2 * chirality + 2]
            out_real = out_imag = None
            for column in range(6):
                c_real = clover[chirality, 0, :, column]
                c_imag = clover[chirality, 1, :, column]
                v_real = pair[column // 3][0][column % 3][None]
                v_imag = pair[column // 3][1][column % 3][None]
                term_real = c_real * v_real - c_imag * v_imag
                term_imag = c_real * v_imag + c_imag * v_real
                out_real = term_real if out_real is None else out_real + term_real
                out_imag = term_imag if out_imag is None else out_imag + term_imag
            result.append((out_real[:3], out_imag[:3]))
            result.append((out_real[3:], out_imag[3:]))
        return tiles_of(result)

    loads[0].wait()
    scaled[...] = fine_relax * source_ref[...]

    def prepare():
        loads[2].wait()
        clover[...] = (fine_relax * kappa_value) * clover_raw[...].astype(F32).reshape(clover.shape)
        loads[3].wait()
        wide[...] = vectors_raw[...].astype(F32).reshape(wide.shape)

    def vector_faces():
        def four(step, carry):
            for k in range(4):
                k = 4 * step + k
                spins = spins_of(wide[k].reshape(24, 8, 128))
                halves = [
                    project(spins, 3, -1),
                    link_times(links, 3, project(spins, 3, 1), True),
                    project(spins, 0, -1),
                    link_times(links, 0, project(spins, 0, 1), True),
                ]
                for part in range(2):
                    if part == 1:
                        halves = [
                            jnp.concatenate([-half[6:], half[:6]], axis=0) for half in halves
                        ]
                    faces[k, part, 0:3] = choose(
                        places.block == 0,
                        pack_slots(halves[0], 3, True, places),
                        pack_slots(halves[1], 3, False, places),
                    )
                    faces[k, part, 3:6] = pack_time(halves[2], True, places)[0]
                    faces[k, part, 6:9] = pack_time(halves[3], False, places)[0]
            return carry

        lax.fori_loop(0, 4, four, 0)

    def enter():
        pl.semaphore_wait(barrier, 6)

    loads[1].wait()
    for load in loads[2:]:
        load.start()
    links[...] = links_raw[...].astype(F32).reshape(links.shape)

    psi = scaled[...]
    psi = (1.0 - fine_relax) * psi + scaled[...] + clover_hopping(0, psi, enter, prepare)

    change = clover_hopping(1, psi, None, vector_faces)
    residual = source_ref[...] - psi + (1.0 / fine_relax) * change

    rounded = residual.astype(BF16).astype(F32)
    rest_real, rest_imag = rounded[:12], rounded[12:]
    reals, imags = [], []
    for k in range(16):
        v_real, v_imag = wide[k, 0], wide[k, 1]
        reals.append(jnp.sum(v_real * rest_real + v_imag * rest_imag, axis=0))
        imags.append(jnp.sum(v_real * rest_imag - v_imag * rest_real, axis=0))

    def over_lanes(tile):
        return jnp.broadcast_to(jnp.sum(tile, axis=-1, keepdims=True), (8, 128))

    def into_lanes(columns):
        layer = list(columns)
        bit = 1
        while len(layer) > 1:
            odd = (places.lane // bit) % 2 == 1
            layer = [
                jnp.where(odd, layer[n + 1], layer[n]) for n in range(0, len(layer), 2)
            ]
            bit *= 2
        return layer[0]

    reals = [over_lanes(tile) for tile in reals]
    imags = [over_lanes(tile) for tile in imags]
    coarse_real, coarse_imag = into_lanes(reals), into_lanes(imags)
    coarse_real = coarse_real + row_roll(coarse_real, 4)
    coarse_imag = coarse_imag + row_roll(coarse_imag, 4)

    own = jnp.where(places.half == 0, coarse_real, coarse_imag)
    coarse_send[...] = own
    coarse_messages = {}
    for number, target in ((1, t_prior), (2, t_next), (0, x_other), (3, y_prior), (4, y_next), (5, z_other)):
        copy = pltpu.make_async_remote_copy(
            src_ref=coarse_send,
            dst_ref=coarse_recv.at[number],
            send_sem=coarse_send_sem.at[number],
            recv_sem=coarse_recv_sem.at[number],
            device_id=target,
            device_id_type=pl.DeviceIdType.MESH,
        )
        copy.start()
        coarse_messages[number] = copy
        started.append(copy)
    settle(6)

    def before_neighbours(total):
        value = total + row_roll(total, 4)
        first = coarse_relax * value
        return first + coarse_relax * (value - first)

    real_bases = [before_neighbours(total) for total in reals]
    imag_bases = [before_neighbours(total) for total in imags]
    loads[4].wait()

    accumulated = [jnp.zeros((8, 8, 16), F32), jnp.zeros((8, 8, 16), F32)]

    def add_hop(number, tile):
        tile = coarse_relax * tile
        swapped = row_roll(tile, 4)
        e_real = jnp.where(places.half == 0, tile, swapped)[:, :16][None]
        e_imag = jnp.where(places.half == 0, swapped, tile)[:, :16][None]
        h_real, h_imag = hops_ref[number, 0], hops_ref[number, 1]
        accumulated[0] = accumulated[0] + (h_real * e_real - h_imag * e_imag)
        accumulated[1] = accumulated[1] + (h_real * e_imag + h_imag * e_real)

    coarse_messages[5].wait_recv()
    z_tile = coarse_recv[5]
    add_hop(2, z_tile)
    add_hop(3, z_tile)
    coarse_messages[3].wait_recv()
    add_hop(4, coarse_recv[3])
    coarse_messages[4].wait_recv()
    add_hop(5, coarse_recv[4])
    coarse_messages[0].wait_recv()
    x_tile = coarse_recv[0]
    add_hop(6, jnp.where(places.block == 3, row_roll(x_tile, 3), row_roll(own, -1)))
    add_hop(7, jnp.where(places.block == 0, row_roll(x_tile, -3), row_roll(own, 1)))
    coarse_messages[1].wait_recv()
    add_hop(0, coarse_recv[1])
    coarse_messages[2].wait_recv()
    add_hop(1, coarse_recv[2])

    def errors(bases, values):
        spread = []
        for pair in range(8):
            total = jnp.broadcast_to(
                jnp.sum(values[pair], axis=-1, keepdims=True), (8, 128)
            )
            swapped = row_roll(total, 4)
            spread.append(jnp.where(places.half == 0, total, swapped))
            spread.append(jnp.where(places.half == 0, swapped, total))
        return [bases[k] + coarse_relax * spread[k] for k in range(16)]

    exact_real = errors(real_bases, accumulated[0])
    exact_imag = errors(imag_bases, accumulated[1])

    error_real = [error.astype(BF16).astype(F32) for error in exact_real]
    error_imag = [error.astype(BF16).astype(F32) for error in exact_imag]

    sent = {}
    for number, place, start, target in (
        (0, 0, X_BOTH, x_other),
        (1, 3, T_AHEAD, t_prior),
        (2, 6, T_BEHIND, t_next),
    ):
        face = send_buffer[1, start : start + 3]
        for k in range(16):
            face = face + (
                error_real[k][None] * faces[k, 0, place : place + 3]
                + error_imag[k][None] * faces[k, 1, place : place + 3]
            )
        send_buffer[2, start : start + 3] = face
        sent[number] = message(2, number, start, 3, target)
        sent[number].start()
        started.append(sent[number])

    add_real, add_imag = psi[:12], psi[12:]
    for k in range(16):
        v_real, v_imag = wide[k, 0], wide[k, 1]
        e_real, e_imag = error_real[k][None], error_imag[k][None]
        add_real = add_real + (v_real * e_real - v_imag * e_imag)
        add_imag = add_imag + (v_real * e_imag + v_imag * e_real)
    psi = jnp.concatenate([add_real, add_imag], axis=0)

    def hand_out():
        coarse_ref[0] = into_lanes(exact_real)[:4, :16]
        coarse_ref[1] = into_lanes(exact_imag)[:4, :16]

    for sweep in (2, 3):
        psi = (
            (1.0 - fine_relax) * psi
            + scaled[...]
            + clover_hopping(
                sweep, psi, None, hand_out if sweep == 2 else None, sent if sweep == 2 else ()
            )
        )
    out_ref[...] = psi

    settle(0)


def deliver(out_in, coarse_in, out_ref, coarse_ref, sems):
    copies = [
        pltpu.make_async_copy(out_in, out_ref, sems.at[0]),
        pltpu.make_async_copy(coarse_in, coarse_ref, sems.at[1]),
    ]
    for copy in copies:
        copy.start()
    for copy in copies:
        copy.wait()


def rows_of_eight(values):
    count = values.size // 1024
    return values.reshape(count, 4, 2, 128).transpose(0, 2, 1, 3).reshape(count, 8, 128)


def local(source, gauge_links, clover_inverse, vectors, coarse_hops):
    source_tiles = rows_of_eight(source)
    link_tiles = rows_of_eight(gauge_links).reshape(36, 16, 128)
    clover_tiles = rows_of_eight(clover_inverse).reshape(72, 16, 128)
    vector_tiles = rows_of_eight(vectors).reshape(32, 6, 16, 128)
    hop_tiles = (
        coarse_hops.reshape(8, 2, 16, 16, 4).transpose(0, 1, 2, 4, 3).reshape(8, 2, 8, 8, 16)
    )
    out, coarse = pl.pallas_call(
        kernel,
        out_shape=(
            jax.ShapeDtypeStruct((24, 8, 128), F32),
            jax.ShapeDtypeStruct((2, 4, 16), F32),
        ),
        in_specs=[pl.BlockSpec(memory_space=pltpu.HBM)] * 5,
        out_specs=(
            pl.BlockSpec(memory_space=pltpu.VMEM),
            pl.BlockSpec(memory_space=pltpu.VMEM),
        ),
        scratch_shapes=[
            pltpu.VMEM((24, 8, 128), F32),
            pltpu.VMEM((36, 16, 128), BF16),
            pltpu.VMEM((72, 16, 128), BF16),
            pltpu.VMEM((32, 6, 16, 128), BF16),
            pltpu.VMEM((8, 2, 8, 8, 16), F32),
            pltpu.VMEM((4, 2, 3, 3, 8, 128), F32),
            pltpu.VMEM((2, 2, 6, 6, 8, 128), F32),
            pltpu.VMEM((16, 2, 12, 8, 128), F32),
            pltpu.VMEM((16, 2, 9, 8, 128), F32),
            pltpu.VMEM((24, 8, 128), F32),
            pltpu.VMEM((4, TILES, 8, 128), F32),
            pltpu.VMEM((4, TILES, 8, 128), F32),
            pltpu.VMEM((8, 128), F32),
            pltpu.VMEM((6, 8, 128), F32),
            pltpu.SemaphoreType.DMA((5,)),
            pltpu.SemaphoreType.DMA((4, 6)),
            pltpu.SemaphoreType.DMA((4, 6)),
            pltpu.SemaphoreType.DMA((6,)),
            pltpu.SemaphoreType.DMA((6,)),
        ],
        compiler_params=pltpu.CompilerParams(
            collective_id=0, has_side_effects=True, vmem_limit_bytes=55040 * 1024
        ),
    )(source_tiles, link_tiles, clover_tiles, vector_tiles, hop_tiles)
    out, coarse = pl.pallas_call(
        deliver,
        out_shape=(
            jax.ShapeDtypeStruct((24, 8, 128), F32),
            jax.ShapeDtypeStruct((2, 4, 16), F32),
        ),
        in_specs=[pl.BlockSpec(memory_space=pl.ANY)] * 2,
        out_specs=[pl.BlockSpec(memory_space=pl.ANY)] * 2,
        scratch_shapes=[pltpu.SemaphoreType.DMA((2,))],
        compiler_params=pltpu.CompilerParams(vmem_limit_bytes=1024 * 1024),
    )(out, coarse)
    solution_out = (
        out.reshape(24, 2, 4, 128).transpose(0, 2, 1, 3).reshape(2, 4, 3, 1, 1, 1, 4, 256)
    )
    coarse_out = coarse.transpose(0, 2, 1).reshape(2, 16, 1, 1, 1, 4)
    return solution_out, coarse_out


def solution(mesh):
    return jax.shard_map(
        local,
        mesh=mesh,
        in_specs=(
            P(None, None, None, "ta", "gz", "gy", "gx", None),
            P(None, None, None, None, "ta", "gz", "gy", "gx", None),
            P(None, None, None, None, "ta", "gz", "gy", "gx", None),
            P(None, None, None, None, "ta", "gz", "gy", "gx", None),
            P(None, None, None, None, "ta", "gz", "gy", "gx"),
        ),
        out_specs=(
            P(None, None, None, "ta", "gz", "gy", "gx", None),
            P(None, None, "ta", "gz", "gy", "gx"),
        ),
        check_vma=False,
    )
```

```python
import jax
import jax.numpy as jnp
from jax import lax
from jax.experimental import pallas as pl
from jax.experimental.pallas import tpu as pltpu
from jax.sharding import PartitionSpec as P


kappa_value = 0.125
fine_relax = 0.8
coarse_relax = 0.7

F32 = jnp.float32
BF16 = jnp.bfloat16

B_ROWS = (((0, 0), (1, 0)), ((0, 3), (1, 1)), ((1, 2), (0, 0)), ((1, 3), (0, 3)))
B_ADJOINT_ROWS = (((0, 0), (1, 0)), ((0, 1), (1, 3)), ((1, 0), (0, 2)), ((1, 1), (0, 1)))

T_AHEAD, T_BEHIND, Y_AHEAD, Y_BEHIND, Z_BOTH, X_BOTH = 0, 3, 6, 9, 12, 18
TILES = 21


def plus_unit(target, unit, value):
    if unit == 0:
        return target[0] + value[0], target[1] + value[1]
    if unit == 1:
        return target[0] - value[1], target[1] + value[0]
    if unit == 2:
        return target[0] - value[0], target[1] - value[1]
    return target[0] + value[1], target[1] - value[0]


def project(spins, direction, sign):
    halves = []
    for row in range(2):
        column, unit = B_ROWS[direction][row]
        unit = unit if sign > 0 else (unit + 2) % 4
        halves.append(plus_unit(spins[row], unit, spins[2 + column]))
    return jnp.concatenate([halves[0][0], halves[1][0], halves[0][1], halves[1][1]], axis=0)


def lift(summed, half, direction, sign):
    pair = [(half[0:3], half[6:9]), (half[3:6], half[9:12])]
    result = []
    for row in range(2):
        result.append(plus_unit(summed[row], 0, pair[row]))
    for row in range(2):
        column, unit = B_ADJOINT_ROWS[direction][row]
        unit = unit if sign > 0 else (unit + 2) % 4
        result.append(plus_unit(summed[2 + row], unit, pair[column]))
    return result


def link_times(links, direction, half, dagger):
    real_part = half[:6].reshape(2, 3, 8, 128)
    imag_part = half[6:].reshape(2, 3, 8, 128)
    out_real = out_imag = None
    for b in range(3):
        if dagger:
            u_real, u_imag = links[direction, 0, b], links[direction, 1, b]
        else:
            u_real, u_imag = links[direction, 0, :, b], links[direction, 1, :, b]
        u_real, u_imag = u_real[None], u_imag[None]
        v_real, v_imag = real_part[:, b][:, None], imag_part[:, b][:, None]
        if dagger:
            term_real = u_real * v_real + u_imag * v_imag
            term_imag = u_real * v_imag - u_imag * v_real
        else:
            term_real = u_real * v_real - u_imag * v_imag
            term_imag = u_real * v_imag + u_imag * v_real
        out_real = term_real if out_real is None else out_real + term_real
        out_imag = term_imag if out_imag is None else out_imag + term_imag
    return jnp.concatenate([out_real.reshape(6, 8, 128), out_imag.reshape(6, 8, 128)], axis=0)


def lane_roll(values, shift):
    shift = shift % 128
    return values if shift == 0 else pltpu.roll(values, shift, values.ndim - 1)


def row_roll(values, shift):
    shift = shift % 8
    return values if shift == 0 else pltpu.roll(values, shift, values.ndim - 2)


class Places:
    def __init__(self):
        row = lax.broadcasted_iota(jnp.int32, (8, 128), 0)
        lane = lax.broadcasted_iota(jnp.int32, (8, 128), 1)
        self.row, self.lane = row, lane
        self.block = row % 4
        self.half = row // 4
        self.parity = lane // 64
        self.slot = {1: (lane // 16) % 4, 2: (lane // 4) % 4, 3: lane % 4}


STRIDE = {1: 16, 2: 4, 3: 1}


def choose(mask, first, second):
    return jnp.where(jnp.broadcast_to(mask[None], first.shape), first, second)


def pack_slots(half, direction, ahead, places):
    stride, slot = STRIDE[direction], places.slot[direction]
    fours = half.reshape(3, 4, 8, 128)
    packed = fours[:, 0]
    for k in range(1, 4):
        if ahead:
            packed = choose(slot == k, lane_roll(fours[:, k], stride * k), packed)
        else:
            packed = choose(slot == 3 - k, lane_roll(fours[:, k], -stride * k), packed)
    return packed


def merge_slots(rolled, packed, direction, ahead, places):
    stride, slot = STRIDE[direction], places.slot[direction]
    fours = rolled.reshape(3, 4, 8, 128)
    merged = []
    for k in range(4):
        if ahead:
            merged.append(choose(slot == 3, lane_roll(packed, stride * (3 - k)), fours[:, k]))
        else:
            merged.append(choose(slot == 0, lane_roll(packed, -stride * (3 - k)), fours[:, k]))
    return jnp.stack(merged, axis=1).reshape(12, 8, 128)


def pack_time(half, ahead, places):
    edge = places.parity == (0 if ahead else 1)
    edge_rows = places.half == (0 if ahead else 1)
    pairs = half.reshape(6, 2, 8, 128)
    first, second = pairs[:, 0], lane_roll(pairs[:, 1], 64)
    paired = choose(edge, first, second).reshape(3, 2, 8, 128)
    paired_first, paired_second = paired[:, 0], row_roll(paired[:, 1], 4)
    packed = choose(edge_rows, paired_first, paired_second)
    return packed, (first, second, paired_first, paired_second)


def merge_time(state, packed, ahead, places):
    edge = places.parity == (0 if ahead else 1)
    edge_rows = places.half == (0 if ahead else 1)
    first, second, paired_first, paired_second = state
    next_first = row_roll(choose(edge_rows, packed, paired_first), 4)
    next_second = choose(edge_rows, paired_second, packed)
    moved = jnp.stack([next_first, next_second], axis=1).reshape(6, 8, 128)
    out_first = lane_roll(choose(edge, moved, first), 64)
    out_second = choose(edge, second, moved)
    return jnp.stack([out_first, out_second], axis=1).reshape(12, 8, 128)


def spins_of(values):
    return [(values[3 * s : 3 * s + 3], values[12 + 3 * s : 15 + 3 * s]) for s in range(4)]


def tiles_of(spins):
    return jnp.concatenate([spin[0] for spin in spins] + [spin[1] for spin in spins], axis=0)


def kernel(
    source_hbm,
    links_hbm,
    clover_hbm,
    vectors_hbm,
    hops_hbm,
    out_ref,
    coarse_ref,
    source_ref,
    links_raw,
    clover_raw,
    vectors_raw,
    hops_ref,
    links,
    clover,
    wide,
    faces,
    scaled,
    send_buffer,
    recv_buffer,
    coarse_send,
    coarse_recv,
    load_sem,
    send_sem,
    recv_sem,
    coarse_send_sem,
    coarse_recv_sem,
):
    loads = []
    for index, (origin, target) in enumerate(
        (
            (source_hbm, source_ref),
            (links_hbm, links_raw),
            (clover_hbm, clover_raw),
            (vectors_hbm, vectors_raw),
            (hops_hbm, hops_ref),
        )
    ):
        loads.append(pltpu.make_async_copy(origin, target, load_sem.at[index]))

    def around(axis, step):
        count = lax.axis_size(axis)
        return {axis: lax.rem(lax.axis_index(axis) + (step + count), count)}

    t_next, t_prior = around("ta", 1), around("ta", -1)
    y_next, y_prior = around("gy", 1), around("gy", -1)
    z_other, x_other = around("gz", 1), around("gx", 1)

    barrier = pltpu.get_barrier_semaphore()
    for neighbour in (x_other, t_next, t_prior, y_next, y_prior, z_other):
        pl.semaphore_signal(
            barrier, inc=1, device_id=neighbour, device_id_type=pl.DeviceIdType.MESH
        )

    loads[0].start()
    loads[1].start()
    places = Places()

    def message(sweep, number, start, count, target):
        window = pl.ds(start, count)
        return pltpu.make_async_remote_copy(
            src_ref=send_buffer.at[sweep, window],
            dst_ref=recv_buffer.at[sweep, window],
            send_sem=send_sem.at[sweep, number],
            recv_sem=recv_sem.at[sweep, number],
            device_id=target,
            device_id_type=pl.DeviceIdType.MESH,
        )

    started = []

    def settle(keep):
        while len(started) > keep:
            started.pop(0).wait_send()

    def clover_hopping(sweep, psi, before_send=None, while_waiting=None, sent=()):
        spins = spins_of(psi)
        send = send_buffer.at[sweep]
        recv = recv_buffer.at[sweep]
        ahead, behind, messages = {}, {}, {}

        def halves(mu):
            ahead[mu] = project(spins, mu, -1)
            behind[mu] = link_times(links, mu, project(spins, mu, 1), True)

        def dispatch(number, start, count, target):
            if number in sent:
                messages[number] = sent[number]
                return
            messages[number] = message(sweep, number, start, count, target)
            started.append(messages[number])
            if before_send is None:
                messages[number].start()

        halves(3)
        x_ahead = pack_slots(ahead[3], 3, True, places)
        x_behind = pack_slots(behind[3], 3, False, places)
        if 0 not in sent:
            send[X_BOTH : X_BOTH + 3] = choose(places.block == 0, x_ahead, x_behind)
        dispatch(0, X_BOTH, 3, x_other)
        ahead[0] = project(spins, 0, -1)
        t_ahead, t_ahead_state = pack_time(ahead[0], True, places)
        if 1 not in sent:
            send[T_AHEAD : T_AHEAD + 3] = t_ahead
        dispatch(1, T_AHEAD, 3, t_prior)
        behind[0] = link_times(links, 0, project(spins, 0, 1), True)
        t_behind, t_behind_state = pack_time(behind[0], False, places)
        if 2 not in sent:
            send[T_BEHIND : T_BEHIND + 3] = t_behind
        dispatch(2, T_BEHIND, 3, t_next)
        halves(2)
        send[Y_AHEAD : Y_AHEAD + 3] = pack_slots(ahead[2], 2, True, places)
        dispatch(3, Y_AHEAD, 3, y_prior)
        send[Y_BEHIND : Y_BEHIND + 3] = pack_slots(behind[2], 2, False, places)
        dispatch(4, Y_BEHIND, 3, y_next)
        halves(1)
        send[Z_BOTH : Z_BOTH + 3] = pack_slots(ahead[1], 1, True, places)
        send[Z_BOTH + 3 : Z_BOTH + 6] = pack_slots(behind[1], 1, False, places)
        dispatch(5, Z_BOTH, 6, z_other)
        if before_send is not None:
            before_send()
            for copy in messages.values():
                copy.start()
        settle(6)
        if while_waiting is not None:
            while_waiting()

        ahead_moved = {mu: lane_roll(ahead[mu], -STRIDE[mu]) for mu in (1, 2, 3)}
        behind_moved = {mu: lane_roll(behind[mu], STRIDE[mu]) for mu in (1, 2, 3)}
        zero = jnp.zeros((3, 8, 128), F32)
        summed = [(zero, zero)] * 4

        def finish(summed, mu, from_ahead, from_behind):
            summed = lift(summed, link_times(links, mu, from_ahead, False), mu, -1)
            return lift(summed, from_behind, mu, 1)

        messages[5].wait_recv()
        summed = finish(
            summed,
            1,
            merge_slots(ahead_moved[1], recv[Z_BOTH : Z_BOTH + 3], 1, True, places),
            merge_slots(behind_moved[1], recv[Z_BOTH + 3 : Z_BOTH + 6], 1, False, places),
        )
        messages[3].wait_recv()
        messages[4].wait_recv()
        summed = finish(
            summed,
            2,
            merge_slots(ahead_moved[2], recv[Y_AHEAD : Y_AHEAD + 3], 2, True, places),
            merge_slots(behind_moved[2], recv[Y_BEHIND : Y_BEHIND + 3], 2, False, places),
        )
        messages[0].wait_recv()
        x_recv = recv[X_BOTH : X_BOTH + 3]
        x_from_ahead = choose(places.block == 3, row_roll(x_recv, 3), row_roll(x_ahead, -1))
        x_from_behind = choose(places.block == 0, row_roll(x_recv, -3), row_roll(x_behind, 1))
        summed = finish(
            summed,
            3,
            merge_slots(ahead_moved[3], x_from_ahead, 3, True, places),
            merge_slots(behind_moved[3], x_from_behind, 3, False, places),
        )
        messages[1].wait_recv()
        messages[2].wait_recv()
        summed = finish(
            summed,
            0,
            merge_time(t_ahead_state, recv[T_AHEAD : T_AHEAD + 3], True, places),
            merge_time(t_behind_state, recv[T_BEHIND : T_BEHIND + 3], False, places),
        )

        result = []
        for chirality in range(2):
            pair = summed[2 * chirality : 2 * chirality + 2]
            out_real = out_imag = None
            for column in range(6):
                c_real = clover[chirality, 0, :, column]
                c_imag = clover[chirality, 1, :, column]
                v_real = pair[column // 3][0][column % 3][None]
                v_imag = pair[column // 3][1][column % 3][None]
                term_real = c_real * v_real - c_imag * v_imag
                term_imag = c_real * v_imag + c_imag * v_real
                out_real = term_real if out_real is None else out_real + term_real
                out_imag = term_imag if out_imag is None else out_imag + term_imag
            result.append((out_real[:3], out_imag[:3]))
            result.append((out_real[3:], out_imag[3:]))
        return tiles_of(result)

    loads[0].wait()
    scaled[...] = fine_relax * source_ref[...]

    def prepare():
        loads[2].wait()
        clover[...] = (fine_relax * kappa_value) * clover_raw[...].astype(F32).reshape(clover.shape)
        loads[3].wait()
        wide[...] = vectors_raw[...].astype(F32).reshape(wide.shape)
        vector_faces(0, 2)

    def vector_faces(begin, end):
        def four(step, carry):
            for k in range(4):
                k = 4 * step + k
                spins = spins_of(wide[k].reshape(24, 8, 128))
                halves = [
                    project(spins, 3, -1),
                    link_times(links, 3, project(spins, 3, 1), True),
                    project(spins, 0, -1),
                    link_times(links, 0, project(spins, 0, 1), True),
                ]
                for part in range(2):
                    if part == 1:
                        halves = [
                            jnp.concatenate([-half[6:], half[:6]], axis=0) for half in halves
                        ]
                    faces[k, part, 0:3] = choose(
                        places.block == 0,
                        pack_slots(halves[0], 3, True, places),
                        pack_slots(halves[1], 3, False, places),
                    )
                    faces[k, part, 3:6] = pack_time(halves[2], True, places)[0]
                    faces[k, part, 6:9] = pack_time(halves[3], False, places)[0]
            return carry

        lax.fori_loop(begin, end, four, 0)

    def enter():
        pl.semaphore_wait(barrier, 6)

    loads[1].wait()
    for load in loads[2:]:
        load.start()
    links[...] = links_raw[...].astype(F32).reshape(links.shape)

    psi = scaled[...]
    psi = (1.0 - fine_relax) * psi + scaled[...] + clover_hopping(0, psi, enter, prepare)

    change = clover_hopping(1, psi, None, lambda: vector_faces(2, 4))
    residual = source_ref[...] - psi + (1.0 / fine_relax) * change

    rounded = residual.astype(BF16).astype(F32)
    rest_real, rest_imag = rounded[:12], rounded[12:]
    reals, imags = [], []
    for k in range(16):
        v_real, v_imag = wide[k, 0], wide[k, 1]
        reals.append(jnp.sum(v_real * rest_real + v_imag * rest_imag, axis=0))
        imags.append(jnp.sum(v_real * rest_imag - v_imag * rest_real, axis=0))

    def over_lanes(tile):
        return jnp.broadcast_to(jnp.sum(tile, axis=-1, keepdims=True), (8, 128))

    def into_lanes(columns):
        layer = list(columns)
        bit = 1
        while len(layer) > 1:
            odd = (places.lane // bit) % 2 == 1
            layer = [
                jnp.where(odd, layer[n + 1], layer[n]) for n in range(0, len(layer), 2)
            ]
            bit *= 2
        return layer[0]

    reals = [over_lanes(tile) for tile in reals]
    imags = [over_lanes(tile) for tile in imags]
    coarse_real, coarse_imag = into_lanes(reals), into_lanes(imags)
    coarse_real = coarse_real + row_roll(coarse_real, 4)
    coarse_imag = coarse_imag + row_roll(coarse_imag, 4)

    own = jnp.where(places.half == 0, coarse_real, coarse_imag)
    coarse_send[...] = own
    coarse_messages = {}
    for number, target in ((1, t_prior), (2, t_next), (0, x_other), (3, y_prior), (4, y_next), (5, z_other)):
        copy = pltpu.make_async_remote_copy(
            src_ref=coarse_send,
            dst_ref=coarse_recv.at[number],
            send_sem=coarse_send_sem.at[number],
            recv_sem=coarse_recv_sem.at[number],
            device_id=target,
            device_id_type=pl.DeviceIdType.MESH,
        )
        copy.start()
        coarse_messages[number] = copy
        started.append(copy)
    settle(6)

    def before_neighbours(total):
        value = total + row_roll(total, 4)
        first = coarse_relax * value
        return first + coarse_relax * (value - first)

    real_bases = [before_neighbours(total) for total in reals]
    imag_bases = [before_neighbours(total) for total in imags]
    loads[4].wait()

    accumulated = [jnp.zeros((8, 8, 16), F32), jnp.zeros((8, 8, 16), F32)]

    def add_hop(number, tile):
        tile = coarse_relax * tile
        swapped = row_roll(tile, 4)
        e_real = jnp.where(places.half == 0, tile, swapped)[:, :16][None]
        e_imag = jnp.where(places.half == 0, swapped, tile)[:, :16][None]
        h_real, h_imag = hops_ref[number, 0], hops_ref[number, 1]
        accumulated[0] = accumulated[0] + (h_real * e_real - h_imag * e_imag)
        accumulated[1] = accumulated[1] + (h_real * e_imag + h_imag * e_real)

    coarse_messages[5].wait_recv()
    z_tile = coarse_recv[5]
    add_hop(2, z_tile)
    add_hop(3, z_tile)
    coarse_messages[3].wait_recv()
    add_hop(4, coarse_recv[3])
    coarse_messages[4].wait_recv()
    add_hop(5, coarse_recv[4])
    coarse_messages[0].wait_recv()
    x_tile = coarse_recv[0]
    add_hop(6, jnp.where(places.block == 3, row_roll(x_tile, 3), row_roll(own, -1)))
    add_hop(7, jnp.where(places.block == 0, row_roll(x_tile, -3), row_roll(own, 1)))
    coarse_messages[1].wait_recv()
    add_hop(0, coarse_recv[1])
    coarse_messages[2].wait_recv()
    add_hop(1, coarse_recv[2])

    def errors(bases, values):
        spread = []
        for pair in range(8):
            total = jnp.broadcast_to(
                jnp.sum(values[pair], axis=-1, keepdims=True), (8, 128)
            )
            swapped = row_roll(total, 4)
            spread.append(jnp.where(places.half == 0, total, swapped))
            spread.append(jnp.where(places.half == 0, swapped, total))
        return [bases[k] + coarse_relax * spread[k] for k in range(16)]

    exact_real = errors(real_bases, accumulated[0])
    exact_imag = errors(imag_bases, accumulated[1])

    error_real = [error.astype(BF16).astype(F32) for error in exact_real]
    error_imag = [error.astype(BF16).astype(F32) for error in exact_imag]

    sent = {}
    for number, place, start, target in (
        (0, 0, X_BOTH, x_other),
        (1, 3, T_AHEAD, t_prior),
        (2, 6, T_BEHIND, t_next),
    ):
        face = send_buffer[1, start : start + 3]
        for k in range(16):
            face = face + (
                error_real[k][None] * faces[k, 0, place : place + 3]
                + error_imag[k][None] * faces[k, 1, place : place + 3]
            )
        send_buffer[2, start : start + 3] = face
        sent[number] = message(2, number, start, 3, target)
        sent[number].start()
        started.append(sent[number])

    add_real, add_imag = psi[:12], psi[12:]
    for k in range(16):
        v_real, v_imag = wide[k, 0], wide[k, 1]
        e_real, e_imag = error_real[k][None], error_imag[k][None]
        add_real = add_real + (v_real * e_real - v_imag * e_imag)
        add_imag = add_imag + (v_real * e_imag + v_imag * e_real)
    psi = jnp.concatenate([add_real, add_imag], axis=0)

    def hand_out():
        coarse_ref[0] = into_lanes(exact_real)[:4, :16]
        coarse_ref[1] = into_lanes(exact_imag)[:4, :16]

    for sweep in (2, 3):
        psi = (
            (1.0 - fine_relax) * psi
            + scaled[...]
            + clover_hopping(
                sweep, psi, None, hand_out if sweep == 2 else None, sent if sweep == 2 else ()
            )
        )
    out_ref[...] = psi

    settle(0)


def deliver(out_in, coarse_in, out_ref, coarse_ref, sems):
    copies = [
        pltpu.make_async_copy(out_in, out_ref, sems.at[0]),
        pltpu.make_async_copy(coarse_in, coarse_ref, sems.at[1]),
    ]
    for copy in copies:
        copy.start()
    for copy in copies:
        copy.wait()


def rows_of_eight(values):
    count = values.size // 1024
    return values.reshape(count, 4, 2, 128).transpose(0, 2, 1, 3).reshape(count, 8, 128)


def local(source, gauge_links, clover_inverse, vectors, coarse_hops):
    source_tiles = rows_of_eight(source)
    link_tiles = rows_of_eight(gauge_links).reshape(36, 16, 128)
    clover_tiles = rows_of_eight(clover_inverse).reshape(72, 16, 128)
    vector_tiles = rows_of_eight(vectors).reshape(32, 6, 16, 128)
    hop_tiles = (
        coarse_hops.reshape(8, 2, 16, 16, 4).transpose(0, 1, 2, 4, 3).reshape(8, 2, 8, 8, 16)
    )
    out, coarse = pl.pallas_call(
        kernel,
        out_shape=(
            jax.ShapeDtypeStruct((24, 8, 128), F32),
            jax.ShapeDtypeStruct((2, 4, 16), F32),
        ),
        in_specs=[pl.BlockSpec(memory_space=pltpu.HBM)] * 5,
        out_specs=(
            pl.BlockSpec(memory_space=pltpu.VMEM),
            pl.BlockSpec(memory_space=pltpu.VMEM),
        ),
        scratch_shapes=[
            pltpu.VMEM((24, 8, 128), F32),
            pltpu.VMEM((36, 16, 128), BF16),
            pltpu.VMEM((72, 16, 128), BF16),
            pltpu.VMEM((32, 6, 16, 128), BF16),
            pltpu.VMEM((8, 2, 8, 8, 16), F32),
            pltpu.VMEM((4, 2, 3, 3, 8, 128), F32),
            pltpu.VMEM((2, 2, 6, 6, 8, 128), F32),
            pltpu.VMEM((16, 2, 12, 8, 128), F32),
            pltpu.VMEM((16, 2, 9, 8, 128), F32),
            pltpu.VMEM((24, 8, 128), F32),
            pltpu.VMEM((4, TILES, 8, 128), F32),
            pltpu.VMEM((4, TILES, 8, 128), F32),
            pltpu.VMEM((8, 128), F32),
            pltpu.VMEM((6, 8, 128), F32),
            pltpu.SemaphoreType.DMA((5,)),
            pltpu.SemaphoreType.DMA((4, 6)),
            pltpu.SemaphoreType.DMA((4, 6)),
            pltpu.SemaphoreType.DMA((6,)),
            pltpu.SemaphoreType.DMA((6,)),
        ],
        compiler_params=pltpu.CompilerParams(
            collective_id=0, has_side_effects=True, vmem_limit_bytes=55040 * 1024
        ),
    )(source_tiles, link_tiles, clover_tiles, vector_tiles, hop_tiles)
    out, coarse = pl.pallas_call(
        deliver,
        out_shape=(
            jax.ShapeDtypeStruct((24, 8, 128), F32),
            jax.ShapeDtypeStruct((2, 4, 16), F32),
        ),
        in_specs=[pl.BlockSpec(memory_space=pl.ANY)] * 2,
        out_specs=[pl.BlockSpec(memory_space=pl.ANY)] * 2,
        scratch_shapes=[pltpu.SemaphoreType.DMA((2,))],
        compiler_params=pltpu.CompilerParams(vmem_limit_bytes=1024 * 1024),
    )(out, coarse)
    solution_out = (
        out.reshape(24, 2, 4, 128).transpose(0, 2, 1, 3).reshape(2, 4, 3, 1, 1, 1, 4, 256)
    )
    coarse_out = coarse.transpose(0, 2, 1).reshape(2, 16, 1, 1, 1, 4)
    return solution_out, coarse_out


def solution(mesh):
    return jax.shard_map(
        local,
        mesh=mesh,
        in_specs=(
            P(None, None, None, "ta", "gz", "gy", "gx", None),
            P(None, None, None, None, "ta", "gz", "gy", "gx", None),
            P(None, None, None, None, "ta", "gz", "gy", "gx", None),
            P(None, None, None, None, "ta", "gz", "gy", "gx", None),
            P(None, None, None, None, "ta", "gz", "gy", "gx"),
        ),
        out_specs=(
            P(None, None, None, "ta", "gz", "gy", "gx", None),
            P(None, None, "ta", "gz", "gy", "gx"),
        ),
        check_vma=False,
    )
```
